32 devices in a mesh: dp: 8 (over z, y), head: 2 (over x), pos: 2 (over core).
Axes of the slice: x: 2, y: 2, z: 4, core: 2. Of those that a mesh axis runs over, the one named last changes fastest.
Arguments:
- queries: bfloat16 [192, 128, 1024], P('dp', 'pos', 'head'), may hold values from -28 to 28
- output_gradient: bfloat16 [192, 128, 1024], P('dp', 'pos', 'head'), may hold values from -24 to 24
- prefix_keys: bfloat16 [8, 256, 256], P('dp', 'pos', 'head'), may hold values from -12 to 12
- prefix_values: bfloat16 [8, 256, 256], P('dp', 'pos', 'head'), may hold values from -6 to 6
- tile_prefix: int32 [192, 1], replicated, may hold values from 0 to 7; in each aligned block of 24 rows (0 to 23, 24 to 47, ...) at most 3 rows name the same one
- suffix_lse: float32 [192, 128, 8], P(None, None, 'head'), may hold values from 5 to 12
- suffix_dot: float32 [192, 128, 8], P(None, None, 'head'), may hold values from -64 to 64
Outputs:
- query_grad: bfloat16 [192, 128, 1024], P('dp', 'pos', 'head')
- key_grad: bfloat16 [8, 256, 256], P('dp', 'pos', 'head')
- value_grad: bfloat16 [8, 256, 256], P('dp', 'pos', 'head')
The draws below stay inside these ranges and needn't reach their ends.
Inputs may be any that keep to these rules, and one draw needn't show every extreme that they name: `tile_prefix`: in each aligned block of 24 tiles (the tiles of one dp index) no prefix is named by more than 3 tiles, and some block has a prefix named exactly 3 times.
All inputs are finite; a program needn't handle non-finite values.
Results may differ from the reference program's by a relative error of at most 0.012.
Values may be sent and summed in bfloat16 or wider, within the bound.
A program may use at most 128 MiB of HBM per device.

```python
import math
import jax
import jax.numpy as jnp
import numpy as np
from jax import lax

HEAD_DIM = 128
Q_GROUP = 4
TILE_ROWS = 128
TILES_DP = 24
KV_HEADS = 2
HEADS = 8
PREFIX_LEN = 256
PREFIXES = 8
CAPACITY = 3
TILES = 192


def draw_queries(key, part):
    key = jax.random.fold_in(key, 11)
    full_shape = (TILES, TILE_ROWS, KV_HEADS * Q_GROUP * HEAD_DIM)
    return (2.0 * jnp.clip(jax.random.normal(key, full_shape, jnp.float32), -6.0, 6.0)).astype(jnp.bfloat16)


def draw_prefix_keys(key, part):
    key = jax.random.fold_in(key, 23)
    full_shape = (PREFIXES, PREFIX_LEN, KV_HEADS * HEAD_DIM)
    return jnp.clip(jax.random.normal(key, full_shape, jnp.float32), -6.0, 6.0).astype(jnp.bfloat16)


def levels(key, dims, cuts, least, high):
    loudness, own = 1.0, jax.random.fold_in(key, 6)
    for dim, shards_of in cuts:
        steps = jnp.exp(jax.random.uniform(jax.random.fold_in(own, dim), (shards_of,), jnp.float32, least / len(cuts), high / len(cuts)))
        loudness = loudness * jnp.repeat(steps, dims[dim] // shards_of).reshape([-1 if axis == dim else 1 for axis in range(len(dims))])
    return loudness


def shared_out(key, own, number, rows, count, top, bound, slope):
    ranking = jax.random.permutation(key, count)
    packed, ordinary = shares(count, rows * top, bound, slope, True), shares(count, rows * top, bound, slope, False)
    places = jnp.arange(count)

    def named(sizes, turn):
        used = int((sizes > 0).sum())
        fixed = max(1, used // 4)
        moved = fixed + (places - fixed + turn * (used - fixed)) % max(1, count - fixed)
        return jnp.zeros((count,), jnp.int32).at[ranking[jnp.where(places < fixed, places, moved)]].set(jnp.asarray(sizes, jnp.int32))

    sizes = jnp.where(number % 4 == 0, named(packed, number // 4), named(ordinary, number - number // 4 - 1))
    mixed = jax.random.permutation(jax.random.fold_in(own, 3), count)
    source_of, sink = mixed[0:count // 2 * 2:2], mixed[1:count // 2 * 2:2]
    margin = jnp.minimum(sizes[source_of] - 1, bound - sizes[sink]) // 2
    margin = jnp.where((source_of == ranking[0]) | (sink == ranking[0]) | (sizes[sink] == 0), 0, jnp.maximum(margin, 0))
    moved = jax.random.randint(jax.random.fold_in(own, 4), (count // 2,), 0, 1 << 20) % (margin + 1)
    sizes = sizes.at[source_of].add(-moved).at[sink].add(moved)
    members = jnp.searchsorted(jnp.cumsum(sizes), jnp.arange(rows * top), side="right").astype(jnp.int32)
    table = members.reshape(top, rows).T
    table = table[jax.random.permutation(jax.random.fold_in(own, 1), rows)]
    turn = jax.random.randint(jax.random.fold_in(own, 2), (rows, 1), 0, top)
    return jnp.take_along_axis(table, (jnp.arange(top)[None, :] + turn) % top, axis=1)


def shares(amount, total, most, slope, full):
    loads = [(1 << 20) // math.isqrt(standing ** slope) + 1 for standing in range(1, amount + 1)]
    largest = most if full else min(most, max(-(-total // amount), total * loads[0] // sum(loads)))
    least = 1 if total - largest >= amount - 1 else 0
    holding, rest = [largest] + [least] * (amount - 1), total - largest - least * (amount - 1)
    while rest > 0:
        free = [i for i in range(1, amount) if holding[i] < largest] or [i for i in range(1, amount) if holding[i] < most]
        pool, remaining = sum([loads[i] for i in free]), rest
        for i in free:
            addition = min(most - holding[i], max(1, remaining * loads[i] // pool), rest)
            holding[i] = holding[i] + addition
            rest = rest - addition
    return np.array(holding)


def gaussian(own_key, shape, scale, most, shards=(), kind=jnp.bfloat16):
    entries = scale * jax.random.normal(own_key, shape, jnp.float32)
    if shards:
        entries = entries * levels(own_key, shape, shards, -0.22, 0.18)
    return jnp.clip(entries, -most, most).astype(kind)


def setup_inputs(seed: int = 0) -> dict:
    splits = jax.random.split(jax.random.key(seed), 8)
    queries = draw_queries(jax.random.fold_in(splits[7], 71), 0)
    output_gradient = gaussian(splits[1], (TILES, TILE_ROWS, HEADS * HEAD_DIM), 4.0, 24.0, ((0, 8), (1, 2), (2, 2)))
    prefix_keys = draw_prefix_keys(jax.random.fold_in(splits[7], 71), 0)
    prefix_values = gaussian(splits[3], (PREFIXES, PREFIX_LEN, KV_HEADS * HEAD_DIM), 1.0, 6.0, ((0, 8), (1, 2), (2, 2)))
    tile_prefix_keys = jax.random.split(jax.random.fold_in(splits[4], 1), TILES // TILES_DP)
    tile_prefix_turns = jax.random.permutation(jax.random.fold_in(splits[4], 3), TILES // TILES_DP)
    tile_prefix = jax.vmap(lambda own, number: shared_out(jax.random.fold_in(splits[4], 2), own, number, TILES_DP, PREFIXES, 1, CAPACITY, 2))(tile_prefix_keys, tile_prefix_turns).reshape((TILES, 1))
    suffix_lse = jnp.clip(5.0 + 7.0 * jax.random.uniform(splits[5], (TILES, TILE_ROWS, HEADS), jnp.float32) ** levels(splits[5], (TILES, TILE_ROWS, HEADS), ((2, 2),), -0.2, 0.2), 5.0, 12.0)
    suffix_dot = gaussian(splits[6], (TILES, TILE_ROWS, HEADS), 16.0, 64.0, ((2, 2),), jnp.float32)
    return dict(queries=queries, output_gradient=output_gradient, prefix_keys=prefix_keys, prefix_values=prefix_values, tile_prefix=tile_prefix, suffix_lse=suffix_lse, suffix_dot=suffix_dot)


def reference(queries, output_gradient, prefix_keys, prefix_values, tile_prefix, suffix_lse, suffix_dot):
    scaling = HEAD_DIM ** -0.5

    def tile_step(running, pieces):
        key_total, value_total = running
        tile_query, tile_gradient, prefix_id, lse_in, dot_in = pieces
        prefix_id = prefix_id.astype(jnp.int32)
        key_rows = lax.dynamic_index_in_dim(prefix_keys, prefix_id, 0, keepdims=False)
        value_rows = lax.dynamic_index_in_dim(prefix_values, prefix_id, 0, keepdims=False)
        query_grid = tile_query.astype(jnp.float32).reshape(TILE_ROWS, KV_HEADS, Q_GROUP, HEAD_DIM)
        grad_grid = tile_gradient.astype(jnp.float32).reshape(TILE_ROWS, KV_HEADS, Q_GROUP, HEAD_DIM)
        key_grid = key_rows.astype(jnp.float32).reshape(PREFIX_LEN, KV_HEADS, HEAD_DIM)
        value_grid = value_rows.astype(jnp.float32).reshape(PREFIX_LEN, KV_HEADS, HEAD_DIM)
        scores = jnp.einsum("rgqd,jgd->rgqj", query_grid, key_grid) * scaling
        prob_grad = jnp.einsum("rgqd,jgd->rgqj", grad_grid, value_grid)
        suffix_l = lse_in.reshape(TILE_ROWS, KV_HEADS, Q_GROUP)
        suffix_d = dot_in.reshape(TILE_ROWS, KV_HEADS, Q_GROUP)
        row_top = jnp.maximum(jnp.max(scores, axis=-1), suffix_l)
        row_mass = jnp.exp(suffix_l - row_top) + jnp.sum(jnp.exp(scores - row_top[..., None]), axis=-1)
        row_lse = row_top + jnp.log(row_mass)
        weights = jnp.exp(scores - row_lse[..., None])
        row_delta = jnp.exp(suffix_l - row_lse) * suffix_d + jnp.sum(weights * prob_grad, axis=-1)
        prob_half = weights.astype(jnp.bfloat16)
        score_grad = (weights * (prob_grad - row_delta[..., None])).astype(jnp.bfloat16)
        query_part = jnp.einsum("rgqj,jgd->rgqd", score_grad.astype(jnp.float32), key_grid) * scaling
        key_part = jnp.einsum("rgqj,rgqd->jgd", score_grad.astype(jnp.float32), query_grid) * scaling
        value_part = jnp.einsum("rgqj,rgqd->jgd", prob_half.astype(jnp.float32), grad_grid)
        key_total = key_total.at[prefix_id].add(key_part.reshape(PREFIX_LEN, KV_HEADS * HEAD_DIM))
        value_total = value_total.at[prefix_id].add(value_part.reshape(PREFIX_LEN, KV_HEADS * HEAD_DIM))
        query_out = query_part.reshape(TILE_ROWS, HEADS * HEAD_DIM).astype(jnp.bfloat16)
        return (key_total, value_total), query_out

    zero_sum = jnp.zeros((PREFIXES, PREFIX_LEN, KV_HEADS * HEAD_DIM), jnp.float32)
    (key_total, value_total), query_grad = lax.scan(
        tile_step, (zero_sum, zero_sum),
        (queries, output_gradient, tile_prefix[:, 0], suffix_lse, suffix_dot))
    return query_grad, key_total.astype(jnp.bfloat16), value_total.astype(jnp.bfloat16)
```

```python
import functools
import math

import jax
import jax.numpy as jnp
from jax import lax
from jax.experimental import pallas as pl
from jax.experimental.pallas import tpu as pltpu
from jax.sharding import PartitionSpec as P

MESH = pl.DeviceIdType.MESH
LOG2E = 1.0 / math.log(2.0)


def exchange_kernel(
    cap,
    q_hbm, g_hbm, k_hbm, v_hbm, tp_ref, lse_hbm, dot_hbm,
    dq_hbm, kg_ref, vg_ref,
    q_ref, g_ref, kv, lse_raw, dot_raw, lse_rows, dot_rows, slots, dq_buf,
    part, sib_out, sib_in, par_out, par_in, line_out, line_in,
    in_sem, kv_recv, kv_sib_send, kv_par_send, kv_line_send,
    sib_send, sib_recv, par_send, par_recv, line_send, line_recv, dq_sem,
):
    tiles, rows, width = q_ref.shape
    prefixes, pos_count, _, block, dim = kv.shape
    heads = width // dim
    line = prefixes // 2
    dp, pos = lax.axis_index("dp"), lax.axis_index("pos")
    a, b = dp // 2, lax.rem(dp, 2)
    other = 1 - b
    scaling = dim ** (-0.5)
    full = cap * prefixes == tiles

    def sibling():
        return {"pos": 1 - pos}

    def partner():
        return {"dp": a * 2 + other}

    def along(d):
        return lax.rem(a + d, line)

    def peer(d):
        return {"dp": along(d) * 2 + b}

    base = dp * tiles
    loads = [
        pltpu.make_async_copy(k_hbm.at[0], kv.at[dp, pos, 0], in_sem.at[0]),
        pltpu.make_async_copy(v_hbm.at[0], kv.at[dp, pos, 1], in_sem.at[1]),
        pltpu.make_async_copy(q_hbm, q_ref, in_sem.at[2]),
        pltpu.make_async_copy(g_hbm, g_ref, in_sem.at[3]),
        pltpu.make_async_copy(lse_hbm.at[pl.ds(base, tiles)], lse_raw, in_sem.at[4]),
        pltpu.make_async_copy(dot_hbm.at[pl.ds(base, tiles)], dot_raw, in_sem.at[5]),
    ]
    for load in loads:
        load.start()

    barrier = pltpu.get_barrier_semaphore()
    pl.semaphore_signal(barrier, inc=1, device_id=sibling(), device_id_type=MESH)
    pl.semaphore_signal(barrier, inc=1, device_id=partner(), device_id_type=MESH)
    for d in range(1, line):
        pl.semaphore_signal(barrier, inc=1, device_id=peer(d), device_id_type=MESH)
    pl.semaphore_wait(barrier, line + 1)

    def remote(src, dst, send, recv, device):
        return pltpu.make_async_remote_copy(
            src_ref=src, dst_ref=dst, send_sem=send, recv_sem=recv,
            device_id=device, device_id_type=MESH,
        )

    def kv_copy(p, send, device):
        mine = kv.at[p, pos]
        return remote(mine, mine, send, kv_recv.at[p, pos], device)

    def kv_wait(p, which):
        here = kv.at[p, which]
        remote(here, here, kv_sib_send.at[p], kv_recv.at[p, which], sibling()).wait_recv()

    loads[0].wait()
    loads[1].wait()
    for d in range(1, line):
        kv_copy(dp, kv_line_send.at[d], peer(d)).start()
    kv_copy(dp, kv_par_send.at[0], partner()).start()
    kv_copy(dp, kv_sib_send.at[dp], sibling()).start()

    def find(p, carry):
        def look(i, found):
            t = tiles - 1 - i
            hit = tp_ref[0, base + t] == p
            shifted = (t,) + found[:-1]
            return tuple(jnp.where(hit, new, old) for new, old in zip(shifted, found))

        found = lax.fori_loop(0, tiles, look, (jnp.int32(-1),) * cap, unroll=True)
        for c in range(cap):
            slots[p * cap + c] = found[c]
        return carry

    lax.fori_loop(0, prefixes, find, 0)

    for load in loads[2:]:
        load.wait()
    for raw, flat in ((lse_raw, lse_rows), (dot_raw, dot_rows)):
        pieces = []
        for h in range(heads):
            row = raw[:, h, :]
            piece = row[:, :rows]
            for other_pos in range(1, pos_count):
                piece = jnp.where(
                    pos == other_pos, row[:, other_pos * rows:(other_pos + 1) * rows], piece
                )
            pieces.append(piece)
        flat[...] = jnp.concatenate(pieces, axis=1)

    def stacked(ref, t):
        tile = ref[t]
        return jnp.concatenate([tile[:, h * dim:(h + 1) * dim] for h in range(heads)], axis=0)

    nt = (((1,), (1,)), ((), ()))
    tn = (((0,), (0,)), ((), ()))
    f32 = jnp.float32

    def compute(p):
        keys = jnp.concatenate([kv[p, i, 0] for i in range(pos_count)], axis=0)
        values = jnp.concatenate([kv[p, i, 1] for i in range(pos_count)], axis=0)
        key_sum = value_sum = None
        for c in range(cap):
            named = slots[p * cap + c]
            t = jnp.maximum(named, 0)
            query, grad = stacked(q_ref, t), stacked(g_ref, t)
            scores = lax.dot_general(keys, query, nt, preferred_element_type=f32)
            prob_grad = lax.dot_general(values, grad, nt, preferred_element_type=f32)
            scores = scores * (scaling * LOG2E)
            suffix_l = lse_rows[pl.ds(t, 1), :] * LOG2E
            suffix_d = dot_rows[pl.ds(t, 1), :]
            top = jnp.maximum(jnp.max(scores, axis=0, keepdims=True), suffix_l)
            shifted = jnp.exp2(scores - top)
            suffix_w = jnp.exp2(suffix_l - top)
            mass = jnp.sum(shifted, axis=0, keepdims=True) + suffix_w
            moment = jnp.sum(shifted * prob_grad, axis=0, keepdims=True) + suffix_w * suffix_d
            inverse = 1.0 / mass
            delta = moment * inverse
            if not full:
                inverse = jnp.where(named >= 0, inverse, 0.0)
            weights = shifted * inverse
            probs = weights.astype(jnp.bfloat16)
            score_grad = (weights * (prob_grad - delta)).astype(jnp.bfloat16)
            key_part = jnp.dot(score_grad, query, preferred_element_type=f32)
            value_part = jnp.dot(probs, grad, preferred_element_type=f32)
            key_sum = key_part if c == 0 else key_sum + key_part
            value_sum = value_part if c == 0 else value_sum + value_part
            query_part = lax.dot_general(score_grad, keys, tn, preferred_element_type=f32)
            query_part = (query_part * scaling).astype(jnp.bfloat16)
            for h in range(heads):
                dq_buf[p, c, :, h * dim:(h + 1) * dim] = query_part[h * rows:(h + 1) * rows]
        key_sum = key_sum * scaling
        for i, total in enumerate((key_sum, value_sum)):
            low, high = total[:block], total[block:]
            part[p, i] = jnp.where(pos == 0, low, high)
            sib_out[p, i] = jnp.where(pos == 0, high, low).astype(jnp.bfloat16)
        remote(
            sib_out.at[p], sib_in.at[p], sib_send.at[p], sib_recv.at[p], sibling()
        ).start()
        pltpu.make_async_copy(dq_buf.at[p], dq_hbm.at[p], dq_sem.at[p]).start()

    def sib_copy(p):
        return remote(sib_out.at[p], sib_in.at[p], sib_send.at[p], sib_recv.at[p], sibling())

    def par_copy(d):
        return remote(par_out.at[d], par_in.at[d], par_send.at[d], par_recv.at[d], partner())

    def line_copy(d):
        return remote(line_out.at[d], line_in.at[d], line_send.at[d], line_recv.at[d], peer(d))

    def to_partner(d):
        p = along(d) * 2 + other
        sib_copy(p).wait_recv()
        par_out[d] = (part[p] + sib_in[p].astype(f32)).astype(jnp.bfloat16)
        par_copy(d).start()

    def chip_sum(d):
        p = along(d) * 2 + b
        sib_copy(p).wait_recv()
        par_copy(d).wait_recv()
        return part[p] + sib_in[p].astype(f32) + par_in[d].astype(f32)

    def to_owner(d):
        line_out[d] = chip_sum(d).astype(jnp.bfloat16)
        line_copy(d).start()

    def turn(d, carry):
        own, across = along(d) * 2 + b, along(d) * 2 + other
        kv_wait(own, 1 - pos)
        compute(own)

        @pl.when(d + 1 < line)
        def _():
            p = along(d + 1) * 2 + b
            kv_wait(p, pos)
            kv_copy(p, kv_par_send.at[d + 1], partner()).start()
            kv_copy(p, kv_sib_send.at[p], sibling()).start()

        @pl.when(d >= 1)
        def _():
            to_partner(d - 1)

        kv_wait(across, pos)
        kv_copy(across, kv_sib_send.at[across], sibling()).start()
        kv_wait(across, 1 - pos)
        compute(across)

        @pl.when(d >= 2)
        def _():
            to_owner(d - 1)

        return carry

    lax.fori_loop(0, line, turn, 0)
    to_partner(line - 1)
    if line > 1:
        to_owner(line - 1)
    total = chip_sum(0)
    for d in range(1, line):
        line_copy(d).wait_recv()
        total = total + line_in[d].astype(f32)
    kg_ref[0] = total[0].astype(jnp.bfloat16)
    vg_ref[0] = total[1].astype(jnp.bfloat16)

    for d in range(1, line):
        kv_copy(dp, kv_line_send.at[d], peer(d)).wait_send()
        line_copy(d).wait_send()

    def drain(d, carry):
        kv_copy(along(d) * 2 + b, kv_par_send.at[d], partner()).wait_send()
        par_copy(d).wait_send()
        return carry

    lax.fori_loop(0, line, drain, 0)

    def drain_prefix(p, carry):
        kv_copy(p, kv_sib_send.at[p], sibling()).wait_send()
        sib_copy(p).wait_send()
        pltpu.make_async_copy(dq_buf.at[p], dq_hbm.at[p], dq_sem.at[p]).wait()
        return carry

    lax.fori_loop(0, prefixes, drain_prefix, 0)


def place_kernel(cap, dq_hbm, kg_hbm, vg_hbm, tp_ref, out_hbm, kg_out, vg_out, counts, sem, small):
    tiles = out_hbm.shape[0]
    prefixes = dq_hbm.shape[0]
    base = lax.axis_index("dp") * tiles
    kg_copy = pltpu.make_async_copy(kg_hbm, kg_out, small.at[0])
    vg_copy = pltpu.make_async_copy(vg_hbm, vg_out, small.at[1])
    kg_copy.start()
    vg_copy.start()
    for p in range(prefixes):
        counts[p] = 0

    def place(t, carry):
        p = tp_ref[0, base + t]
        c = counts[p]
        counts[p] = c + 1
        pltpu.make_async_copy(dq_hbm.at[p, c], out_hbm.at[t], sem.at[t]).start()
        return carry

    def finish(t, carry):
        pltpu.make_async_copy(dq_hbm.at[0, 0], out_hbm.at[t], sem.at[t]).wait()
        return carry

    lax.fori_loop(0, tiles, place, 0)
    lax.fori_loop(0, tiles, finish, 0)
    kg_copy.wait()
    vg_copy.wait()


def shards(
    queries, output_gradient, prefix_keys, prefix_values, tile_prefix, suffix_lse, suffix_dot
):
    prefixes = lax.axis_size("dp")
    pos_count = lax.axis_size("pos")
    tiles, rows, width = queries.shape
    _, block, dim = prefix_keys.shape
    heads = width // dim
    tile_rows = rows * pos_count
    cap = max(2, tiles // prefixes)
    line = prefixes // 2
    bf16, f32 = jnp.bfloat16, jnp.float32
    named = tile_prefix.T
    any_spec = pl.BlockSpec(memory_space=pl.ANY)
    smem_spec = pl.BlockSpec(memory_space=pltpu.SMEM)
    vmem_spec = pl.BlockSpec(memory_space=pltpu.VMEM)
    dma = pltpu.SemaphoreType.DMA
    pair = (2, block, dim)
    work = 10 * tiles * rows * width * block * pos_count
    dq, kg, vg = pl.pallas_call(
        functools.partial(exchange_kernel, cap),
        out_shape=(
            jax.ShapeDtypeStruct((prefixes, cap, rows, width), bf16),
            jax.ShapeDtypeStruct(prefix_keys.shape, bf16),
            jax.ShapeDtypeStruct(prefix_values.shape, bf16),
        ),
        in_specs=[any_spec] * 4 + [smem_spec] + [any_spec] * 2,
        out_specs=(any_spec, vmem_spec, vmem_spec),
        scratch_shapes=[
            pltpu.VMEM((tiles, rows, width), bf16),
            pltpu.VMEM((tiles, rows, width), bf16),
            pltpu.VMEM((prefixes, pos_count) + pair, bf16),
            pltpu.VMEM((tiles, heads, tile_rows), f32),
            pltpu.VMEM((tiles, heads, tile_rows), f32),
            pltpu.VMEM((tiles, heads * rows), f32),
            pltpu.VMEM((tiles, heads * rows), f32),
            pltpu.SMEM((prefixes * cap,), jnp.int32),
            pltpu.VMEM((prefixes, cap, rows, width), bf16),
            pltpu.VMEM((prefixes,) + pair, f32),
            pltpu.VMEM((prefixes,) + pair, bf16),
            pltpu.VMEM((prefixes,) + pair, bf16),
            pltpu.VMEM((line,) + pair, bf16),
            pltpu.VMEM((line,) + pair, bf16),
            pltpu.VMEM((line,) + pair, bf16),
            pltpu.VMEM((line,) + pair, bf16),
            dma((6,)),
            dma((prefixes, pos_count)),
            dma((prefixes,)),
            dma((line,)),
            dma((line,)),
            dma((prefixes,)),
            dma((prefixes,)),
            dma((line,)),
            dma((line,)),
            dma((line,)),
            dma((line,)),
            dma((prefixes,)),
        ],
        compiler_params=pltpu.CompilerParams(
            collective_id=0, has_side_effects=True, vmem_limit_bytes=48 << 20
        ),
        cost_estimate=pl.CostEstimate(
            flops=work, bytes_accessed=6 * tiles * rows * width, transcendentals=0
        ),
        name="prefix_grads",
    )(
        queries, output_gradient, prefix_keys, prefix_values, named,
        jnp.swapaxes(suffix_lse, 1, 2), jnp.swapaxes(suffix_dot, 1, 2),
    )
    return pl.pallas_call(
        functools.partial(place_kernel, cap),
        out_shape=(
            jax.ShapeDtypeStruct(queries.shape, bf16),
            jax.ShapeDtypeStruct(prefix_keys.shape, bf16),
            jax.ShapeDtypeStruct(prefix_values.shape, bf16),
        ),
        in_specs=[any_spec] * 3 + [smem_spec],
        out_specs=(any_spec,) * 3,
        scratch_shapes=[pltpu.SMEM((prefixes,), jnp.int32), dma((tiles,)), dma((2,))],
        name="place_tiles",
    )(dq, kg, vg, named)


def solution(mesh):
    in_specs = (
        P("dp", "pos", "head"),
        P("dp", "pos", "head"),
        P("dp", "pos", "head"),
        P("dp", "pos", "head"),
        P(),
        P(None, None, "head"),
        P(None, None, "head"),
    )
    out_specs = (P("dp", "pos", "head"), P("dp", "pos", "head"), P("dp", "pos", "head"))
    return jax.shard_map(shards, mesh=mesh, in_specs=in_specs, out_specs=out_specs, check_vma=False)
```

```python
import functools
import math

import jax
import jax.numpy as jnp
from jax import lax
from jax.experimental import pallas as pl
from jax.experimental.pallas import tpu as pltpu
from jax.sharding import PartitionSpec as P

MESH = pl.DeviceIdType.MESH
LOG2E = 1.0 / math.log(2.0)


def exchange_kernel(
    cap,
    q_hbm, g_hbm, k_hbm, v_hbm, tp_hbm, lse_hbm, dot_hbm,
    dq_ref, kg_ref, vg_ref,
    tp_ref, q_ref, g_ref, kv, lse_raw, dot_raw, lse_rows, dot_rows, slots,
    part, sib_out, sib_in, par_out, par_in, line_out, line_in,
    in_sem, kv_recv, kv_sib_send, kv_par_send, kv_line_send,
    sib_send, sib_recv, par_send, par_recv, line_send, line_recv,
):
    tiles, rows, width = q_ref.shape
    prefixes, pos_count, _, block, dim = kv.shape
    heads = width // dim
    line = prefixes // 2
    dp, pos = lax.axis_index("dp"), lax.axis_index("pos")
    a, b = dp // 2, lax.rem(dp, 2)
    other = 1 - b
    scaling = dim ** (-0.5)
    full = cap * prefixes == tiles

    def sibling():
        return {"pos": 1 - pos}

    def partner():
        return {"dp": a * 2 + other}

    def along(d):
        return lax.rem(a + d, line)

    def peer(d):
        return {"dp": along(d) * 2 + b}

    base = dp * tiles
    loads = [
        pltpu.make_async_copy(k_hbm.at[0], kv.at[dp, pos, 0], in_sem.at[0]),
        pltpu.make_async_copy(v_hbm.at[0], kv.at[dp, pos, 1], in_sem.at[1]),
        pltpu.make_async_copy(q_hbm, q_ref, in_sem.at[2]),
        pltpu.make_async_copy(g_hbm, g_ref, in_sem.at[3]),
        pltpu.make_async_copy(lse_hbm.at[pl.ds(base, tiles)], lse_raw, in_sem.at[4]),
        pltpu.make_async_copy(dot_hbm.at[pl.ds(base, tiles)], dot_raw, in_sem.at[5]),
        pltpu.make_async_copy(tp_hbm, tp_ref, in_sem.at[6]),
    ]
    for load in loads:
        load.start()

    barrier = pltpu.get_barrier_semaphore()
    pl.semaphore_signal(barrier, inc=1, device_id=sibling(), device_id_type=MESH)
    pl.semaphore_signal(barrier, inc=1, device_id=partner(), device_id_type=MESH)
    for d in range(1, line):
        pl.semaphore_signal(barrier, inc=1, device_id=peer(d), device_id_type=MESH)
    pl.semaphore_wait(barrier, line + 1)

    def remote(src, dst, send, recv, device):
        return pltpu.make_async_remote_copy(
            src_ref=src, dst_ref=dst, send_sem=send, recv_sem=recv,
            device_id=device, device_id_type=MESH,
        )

    def kv_copy(p, send, device):
        mine = kv.at[p, pos]
        return remote(mine, mine, send, kv_recv.at[p, pos], device)

    def kv_wait(p, which):
        here = kv.at[p, which]
        remote(here, here, kv_sib_send.at[p], kv_recv.at[p, which], sibling()).wait_recv()

    loads[0].wait()
    loads[1].wait()
    for d in range(1, line):
        kv_copy(dp, kv_line_send.at[d], peer(d)).start()
    kv_copy(dp, kv_par_send.at[0], partner()).start()
    kv_copy(dp, kv_sib_send.at[dp], sibling()).start()

    loads[6].wait()

    def find(p, carry):
        def look(i, found):
            t = tiles - 1 - i
            hit = tp_ref[0, base + t] == p
            shifted = (t,) + found[:-1]
            return tuple(jnp.where(hit, new, old) for new, old in zip(shifted, found))

        found = lax.fori_loop(0, tiles, look, (jnp.int32(-1),) * cap, unroll=True)
        for c in range(cap):
            slots[p * cap + c] = found[c]
        return carry

    lax.fori_loop(0, prefixes, find, 0)

    for load in loads[2:6]:
        load.wait()
    for raw, flat in ((lse_raw, lse_rows), (dot_raw, dot_rows)):
        pieces = []
        for h in range(heads):
            row = raw[:, h, :]
            piece = row[:, :rows]
            for other_pos in range(1, pos_count):
                piece = jnp.where(
                    pos == other_pos, row[:, other_pos * rows:(other_pos + 1) * rows], piece
                )
            pieces.append(piece)
        flat[...] = jnp.concatenate(pieces, axis=1)

    def stacked(ref, t):
        tile = ref[t]
        return jnp.concatenate([tile[:, h * dim:(h + 1) * dim] for h in range(heads)], axis=0)

    nt = (((1,), (1,)), ((), ()))
    f32 = jnp.float32

    def compute(p):
        keys = jnp.concatenate([kv[p, i, 0] for i in range(pos_count)], axis=0)
        values = jnp.concatenate([kv[p, i, 1] for i in range(pos_count)], axis=0)
        keys_t = keys.T
        key_sum = value_sum = None
        for c in range(cap):
            named = slots[p * cap + c]
            t = jnp.maximum(named, 0)
            query, grad = stacked(q_ref, t), stacked(g_ref, t)
            scores = lax.dot_general(keys, query, nt, preferred_element_type=f32)
            prob_grad = lax.dot_general(values, grad, nt, preferred_element_type=f32)
            scores = scores * (scaling * LOG2E)
            suffix_l = lse_rows[pl.ds(t, 1), :] * LOG2E
            suffix_d = dot_rows[pl.ds(t, 1), :]
            top = jnp.maximum(jnp.max(scores, axis=0, keepdims=True), suffix_l)
            shifted = jnp.exp2(scores - top)
            suffix_w = jnp.exp2(suffix_l - top)
            mass = jnp.sum(shifted, axis=0, keepdims=True) + suffix_w
            moment = jnp.sum(shifted * prob_grad, axis=0, keepdims=True) + suffix_w * suffix_d
            inverse = 1.0 / mass
            delta = moment * inverse
            if not full:
                inverse = jnp.where(named >= 0, inverse, 0.0)
            weights = shifted * inverse
            probs = weights.astype(jnp.bfloat16)
            score_grad = (weights * (prob_grad - delta)).astype(jnp.bfloat16)
            key_part = jnp.dot(score_grad, query, preferred_element_type=f32)
            value_part = jnp.dot(probs, grad, preferred_element_type=f32)
            key_sum = key_part if c == 0 else key_sum + key_part
            value_sum = value_part if c == 0 else value_sum + value_part
            query_part = jnp.dot(keys_t, score_grad, preferred_element_type=f32)
            query_part = (query_part * scaling).T.astype(jnp.bfloat16)
            for h in range(heads):
                dq_ref[p, c, :, h * dim:(h + 1) * dim] = query_part[h * rows:(h + 1) * rows]
        key_sum = key_sum * scaling
        for i, total in enumerate((key_sum, value_sum)):
            low, high = total[:block], total[block:]
            part[p, i] = jnp.where(pos == 0, low, high)
            sib_out[p, i] = jnp.where(pos == 0, high, low).astype(jnp.bfloat16)
        remote(
            sib_out.at[p], sib_in.at[p], sib_send.at[p], sib_recv.at[p], sibling()
        ).start()

    def sib_copy(p):
        return remote(sib_out.at[p], sib_in.at[p], sib_send.at[p], sib_recv.at[p], sibling())

    def par_copy(d):
        return remote(par_out.at[d], par_in.at[d], par_send.at[d], par_recv.at[d], partner())

    def line_copy(d):
        return remote(line_out.at[d], line_in.at[d], line_send.at[d], line_recv.at[d], peer(d))

    def to_partner(d):
        p = along(d) * 2 + other
        sib_copy(p).wait_recv()
        par_out[d] = (part[p] + sib_in[p].astype(f32)).astype(jnp.bfloat16)
        par_copy(d).start()

    def chip_sum(d):
        p = along(d) * 2 + b
        sib_copy(p).wait_recv()
        par_copy(d).wait_recv()
        return part[p] + sib_in[p].astype(f32) + par_in[d].astype(f32)

    def to_owner(d):
        line_out[d] = chip_sum(d).astype(jnp.bfloat16)
        line_copy(d).start()

    def turn(d, carry):
        own, across = along(d) * 2 + b, along(d) * 2 + other
        kv_wait(own, 1 - pos)
        compute(own)

        @pl.when(d + 1 < line)
        def _():
            p = along(d + 1) * 2 + b
            kv_wait(p, pos)
            kv_copy(p, kv_par_send.at[d + 1], partner()).start()
            kv_copy(p, kv_sib_send.at[p], sibling()).start()

        @pl.when(d >= 1)
        def _():
            to_partner(d - 1)

        kv_wait(across, pos)
        kv_copy(across, kv_sib_send.at[across], sibling()).start()
        kv_wait(across, 1 - pos)
        compute(across)

        @pl.when(d >= 2)
        def _():
            to_owner(d - 1)

        return carry

    lax.fori_loop(0, line, turn, 0)
    to_partner(line - 1)
    if line > 1:
        to_owner(line - 1)
    total = chip_sum(0)
    for d in range(1, line):
        line_copy(d).wait_recv()
        total = total + line_in[d].astype(f32)
    kg_ref[0] = total[0].astype(jnp.bfloat16)
    vg_ref[0] = total[1].astype(jnp.bfloat16)

    for d in range(1, line):
        kv_copy(dp, kv_line_send.at[d], peer(d)).wait_send()
        line_copy(d).wait_send()

    def drain(d, carry):
        kv_copy(along(d) * 2 + b, kv_par_send.at[d], partner()).wait_send()
        par_copy(d).wait_send()
        return carry

    lax.fori_loop(0, line, drain, 0)

    def drain_prefix(p, carry):
        kv_copy(p, kv_sib_send.at[p], sibling()).wait_send()
        sib_copy(p).wait_send()
        return carry

    lax.fori_loop(0, prefixes, drain_prefix, 0)


def place_kernel(cap, dq_ref, kg_ref, vg_ref, tp_ref, out_hbm, kg_out, vg_out, counts, sem, small):
    tiles = out_hbm.shape[0]
    prefixes = dq_ref.shape[0]
    base = lax.axis_index("dp") * tiles
    kg_copy = pltpu.make_async_copy(kg_ref, kg_out, small.at[0])
    vg_copy = pltpu.make_async_copy(vg_ref, vg_out, small.at[1])
    kg_copy.start()
    vg_copy.start()
    for p in range(prefixes):
        counts[p] = 0

    def place(t, carry):
        p = tp_ref[0, base + t]
        c = counts[p]
        counts[p] = c + 1
        pltpu.make_async_copy(dq_ref.at[p, c], out_hbm.at[t], sem.at[t]).start()
        return carry

    def finish(t, carry):
        pltpu.make_async_copy(dq_ref.at[0, 0], out_hbm.at[t], sem.at[t]).wait()
        return carry

    lax.fori_loop(0, tiles, place, 0)
    lax.fori_loop(0, tiles, finish, 0)
    kg_copy.wait()
    vg_copy.wait()


def stay(array):
    return pltpu.with_memory_space_constraint(array, pltpu.HBM)


def shards(
    queries, output_gradient, prefix_keys, prefix_values, tile_prefix, suffix_lse, suffix_dot
):
    prefixes = lax.axis_size("dp")
    pos_count = lax.axis_size("pos")
    tiles, rows, width = queries.shape
    _, block, dim = prefix_keys.shape
    heads = width // dim
    tile_rows = rows * pos_count
    cap = max(2, tiles // prefixes)
    line = prefixes // 2
    bf16, f32 = jnp.bfloat16, jnp.float32
    named = stay(tile_prefix.T)
    hbm_spec = pl.BlockSpec(memory_space=pltpu.HBM)
    smem_spec = pl.BlockSpec(memory_space=pltpu.SMEM)
    vmem_spec = pl.BlockSpec(memory_space=pltpu.VMEM)
    dma = pltpu.SemaphoreType.DMA
    pair = (2, block, dim)
    work = 10 * tiles * rows * width * block * pos_count
    dq, kg, vg = pl.pallas_call(
        functools.partial(exchange_kernel, cap),
        out_shape=(
            jax.ShapeDtypeStruct((prefixes, cap, rows, width), bf16),
            jax.ShapeDtypeStruct(prefix_keys.shape, bf16),
            jax.ShapeDtypeStruct(prefix_values.shape, bf16),
        ),
        in_specs=[hbm_spec] * 7,
        out_specs=(vmem_spec, vmem_spec, vmem_spec),
        scratch_shapes=[
            pltpu.SMEM(named.shape, jnp.int32),
            pltpu.VMEM((tiles, rows, width), bf16),
            pltpu.VMEM((tiles, rows, width), bf16),
            pltpu.VMEM((prefixes, pos_count) + pair, bf16),
            pltpu.VMEM((tiles, heads, tile_rows), f32),
            pltpu.VMEM((tiles, heads, tile_rows), f32),
            pltpu.VMEM((tiles, heads * rows), f32),
            pltpu.VMEM((tiles, heads * rows), f32),
            pltpu.SMEM((prefixes * cap,), jnp.int32),
            pltpu.VMEM((prefixes,) + pair, f32),
            pltpu.VMEM((prefixes,) + pair, bf16),
            pltpu.VMEM((prefixes,) + pair, bf16),
            pltpu.VMEM((line,) + pair, bf16),
            pltpu.VMEM((line,) + pair, bf16),
            pltpu.VMEM((line,) + pair, bf16),
            pltpu.VMEM((line,) + pair, bf16),
            dma((7,)),
            dma((prefixes, pos_count)),
            dma((prefixes,)),
            dma((line,)),
            dma((line,)),
            dma((prefixes,)),
            dma((prefixes,)),
            dma((line,)),
            dma((line,)),
            dma((line,)),
            dma((line,)),
        ],
        compiler_params=pltpu.CompilerParams(
            collective_id=0, has_side_effects=True, vmem_limit_bytes=48 << 20
        ),
        cost_estimate=pl.CostEstimate(
            flops=work, bytes_accessed=6 * tiles * rows * width, transcendentals=0
        ),
        name="prefix_grads",
    )(
        stay(queries), stay(output_gradient), stay(prefix_keys), stay(prefix_values), named,
        stay(jnp.swapaxes(suffix_lse, 1, 2)), stay(jnp.swapaxes(suffix_dot, 1, 2)),
    )
    return pl.pallas_call(
        functools.partial(place_kernel, cap),
        out_shape=(
            jax.ShapeDtypeStruct(queries.shape, bf16),
            jax.ShapeDtypeStruct(prefix_keys.shape, bf16),
            jax.ShapeDtypeStruct(prefix_values.shape, bf16),
        ),
        in_specs=[vmem_spec] * 3 + [smem_spec],
        out_specs=(hbm_spec,) * 3,
        scratch_shapes=[pltpu.SMEM((prefixes,), jnp.int32), dma((tiles,)), dma((2,))],
        compiler_params=pltpu.CompilerParams(vmem_limit_bytes=16 << 20),
        name="place_tiles",
    )(dq, kg, vg, named)


def solution(mesh):
    in_specs = (
        P("dp", "pos", "head"),
        P("dp", "pos", "head"),
        P("dp", "pos", "head"),
        P("dp", "pos", "head"),
        P(),
        P(None, None, "head"),
        P(None, None, "head"),
    )
    out_specs = (P("dp", "pos", "head"), P("dp", "pos", "head"), P("dp", "pos", "head"))
    return jax.shard_map(shards, mesh=mesh, in_specs=in_specs, out_specs=out_specs, check_vma=False)
```

```python
import functools
import math

import jax
import jax.numpy as jnp
from jax import lax
from jax.experimental import pallas as pl
from jax.experimental.pallas import tpu as pltpu
from jax.sharding import PartitionSpec as P

MESH = pl.DeviceIdType.MESH
LOG2E = 1.0 / math.log(2.0)


def exchange_kernel(
    cap,
    q_hbm, g_hbm, k_hbm, v_hbm, tp_hbm, lse_hbm, dot_hbm,
    dq_ref, kg_ref, vg_ref,
    tp_ref, q_ref, g_ref, kv, lse_raw, dot_raw, lse_rows, dot_rows, slots,
    part, sib_out, sib_in, par_out, par_in, line_out, line_in,
    in_sem, kv_recv, kv_sib_send, kv_par_send, kv_line_send,
    sib_send, sib_recv, par_send, par_recv, line_send, line_recv,
):
    tiles, rows, width = q_ref.shape
    prefixes, pos_count, _, block, dim = kv.shape
    heads = width // dim
    line = prefixes // 2
    dp, pos = lax.axis_index("dp"), lax.axis_index("pos")
    a, b = dp // 2, lax.rem(dp, 2)
    other = 1 - b
    scaling = dim ** (-0.5)
    full = cap * prefixes == tiles

    def sibling():
        return {"pos": 1 - pos}

    def partner():
        return {"dp": a * 2 + other}

    def along(d):
        return lax.rem(a + d, line)

    def peer(d):
        return {"dp": along(d) * 2 + b}

    base = dp * tiles
    loads = [
        pltpu.make_async_copy(k_hbm.at[0], kv.at[dp, pos, 0], in_sem.at[0]),
        pltpu.make_async_copy(v_hbm.at[0], kv.at[dp, pos, 1], in_sem.at[1]),
        pltpu.make_async_copy(q_hbm, q_ref, in_sem.at[2]),
        pltpu.make_async_copy(g_hbm, g_ref, in_sem.at[3]),
        pltpu.make_async_copy(lse_hbm.at[pl.ds(base, tiles)], lse_raw, in_sem.at[4]),
        pltpu.make_async_copy(dot_hbm.at[pl.ds(base, tiles)], dot_raw, in_sem.at[5]),
        pltpu.make_async_copy(tp_hbm, tp_ref, in_sem.at[6]),
    ]
    for load in loads:
        load.start()

    barrier = pltpu.get_barrier_semaphore()
    pl.semaphore_signal(barrier, inc=1, device_id=sibling(), device_id_type=MESH)
    pl.semaphore_signal(barrier, inc=1, device_id=partner(), device_id_type=MESH)
    for d in range(1, line):
        pl.semaphore_signal(barrier, inc=1, device_id=peer(d), device_id_type=MESH)
    pl.semaphore_wait(barrier, line + 1)

    def remote(src, dst, send, recv, device):
        return pltpu.make_async_remote_copy(
            src_ref=src, dst_ref=dst, send_sem=send, recv_sem=recv,
            device_id=device, device_id_type=MESH,
        )

    def kv_copy(p, send, device):
        mine = kv.at[p, pos]
        return remote(mine, mine, send, kv_recv.at[p, pos], device)

    def kv_wait(p, which):
        here = kv.at[p, which]
        remote(here, here, kv_sib_send.at[p], kv_recv.at[p, which], sibling()).wait_recv()

    loads[0].wait()
    loads[1].wait()
    for d in range(1, line):
        kv_copy(dp, kv_line_send.at[d], peer(d)).start()
    kv_copy(dp, kv_par_send.at[0], partner()).start()
    kv_copy(dp, kv_sib_send.at[dp], sibling()).start()

    loads[6].wait()

    def find(p, carry):
        def look(i, found):
            t = tiles - 1 - i
            hit = tp_ref[0, base + t] == p
            shifted = (t,) + found[:-1]
            return tuple(jnp.where(hit, new, old) for new, old in zip(shifted, found))

        found = lax.fori_loop(0, tiles, look, (jnp.int32(-1),) * cap, unroll=True)
        for c in range(cap):
            slots[p * cap + c] = found[c]
        return carry

    lax.fori_loop(0, prefixes, find, 0)

    for load in loads[2:6]:
        load.wait()
    for raw, flat in ((lse_raw, lse_rows), (dot_raw, dot_rows)):
        pieces = []
        for h in range(heads):
            row = raw[:, h, :]
            piece = row[:, :rows]
            for other_pos in range(1, pos_count):
                piece = jnp.where(
                    pos == other_pos, row[:, other_pos * rows:(other_pos + 1) * rows], piece
                )
            pieces.append(piece)
        flat[...] = jnp.concatenate(pieces, axis=1)

    def stacked(ref, t):
        tile = ref[t]
        return jnp.concatenate([tile[:, h * dim:(h + 1) * dim] for h in range(heads)], axis=0)

    nt = (((1,), (1,)), ((), ()))
    f32 = jnp.float32

    def compute(p):
        keys = jnp.concatenate([kv[p, i, 0] for i in range(pos_count)], axis=0)
        values = jnp.concatenate([kv[p, i, 1] for i in range(pos_count)], axis=0)
        named = [slots[p * cap + c] for c in range(cap)]
        found = [jnp.maximum(t, 0) for t in named]
        query = [stacked(q_ref, t) for t in found]
        grad = [stacked(g_ref, t) for t in found]
        probs, score_grad = [], []
        for c in range(cap):
            scores = lax.dot_general(keys, query[c], nt, preferred_element_type=f32)
            prob_grad = lax.dot_general(values, grad[c], nt, preferred_element_type=f32)
            suffix_l = lse_rows[pl.ds(found[c], 1), :] * LOG2E
            suffix_d = dot_rows[pl.ds(found[c], 1), :]
            scores = scores * (scaling * LOG2E)
            top = jnp.maximum(jnp.max(scores, axis=0, keepdims=True), suffix_l)
            shifted = jnp.exp2(scores - top)
            suffix_w = jnp.exp2(suffix_l - top)
            mass = jnp.sum(shifted, axis=0, keepdims=True) + suffix_w
            moment = jnp.sum(shifted * prob_grad, axis=0, keepdims=True) + suffix_w * suffix_d
            inverse = 1.0 / mass
            delta = moment * inverse
            if not full:
                inverse = jnp.where(named[c] >= 0, inverse, 0.0)
            weights = shifted * inverse
            probs.append(weights.astype(jnp.bfloat16))
            score_grad.append((weights * (prob_grad - delta)).astype(jnp.bfloat16))
        probs = jnp.concatenate(probs, axis=1)
        score_grad = jnp.concatenate(score_grad, axis=1)
        value_sum = jnp.dot(probs, jnp.concatenate(grad, axis=0), preferred_element_type=f32)
        key_sum = jnp.dot(score_grad, jnp.concatenate(query, axis=0), preferred_element_type=f32)
        key_sum = key_sum * scaling
        for i, total in enumerate((key_sum, value_sum)):
            low, high = total[:block], total[block:]
            part[p, i] = jnp.where(pos == 0, low, high)
            sib_out[p, i] = jnp.where(pos == 0, high, low).astype(jnp.bfloat16)
        remote(
            sib_out.at[p], sib_in.at[p], sib_send.at[p], sib_recv.at[p], sibling()
        ).start()
        query_part = jnp.dot(keys.T, score_grad, preferred_element_type=f32)
        query_part = (query_part * scaling).astype(jnp.bfloat16).T
        for c in range(cap):
            for h in range(heads):
                first = (c * heads + h) * rows
                dq_ref[p, c, :, h * dim:(h + 1) * dim] = query_part[first:first + rows]

    def sib_copy(p):
        return remote(sib_out.at[p], sib_in.at[p], sib_send.at[p], sib_recv.at[p], sibling())

    def par_copy(d):
        return remote(par_out.at[d], par_in.at[d], par_send.at[d], par_recv.at[d], partner())

    def line_copy(d):
        return remote(line_out.at[d], line_in.at[d], line_send.at[d], line_recv.at[d], peer(d))

    def to_partner(d):
        p = along(d) * 2 + other
        sib_copy(p).wait_recv()
        par_out[d] = (part[p] + sib_in[p].astype(f32)).astype(jnp.bfloat16)
        par_copy(d).start()

    def chip_sum(d):
        p = along(d) * 2 + b
        sib_copy(p).wait_recv()
        par_copy(d).wait_recv()
        return part[p] + sib_in[p].astype(f32) + par_in[d].astype(f32)

    def to_owner(d):
        line_out[d] = chip_sum(d).astype(jnp.bfloat16)
        line_copy(d).start()

    def forward_along(d):
        p = along(d) * 2 + b
        kv_wait(p, pos)
        kv_copy(p, kv_par_send.at[d], partner()).start()
        kv_copy(p, kv_sib_send.at[p], sibling()).start()

    def forward_across(d):
        p = along(d) * 2 + other
        kv_wait(p, pos)
        kv_copy(p, kv_sib_send.at[p], sibling()).start()

    def step(s, carry):
        half = (s + 1) // 2
        odd = lax.rem(s, 2) == 1
        across = ((s > 0) & (lax.rem(s, 2) == 0)) | (s == 2 * line - 1)
        p = along(lax.rem(half, line)) * 2 + jnp.where(across, other, b)
        kv_wait(p, 1 - pos)
        compute(p)

        @pl.when(s == 0)
        def _():
            if line > 1:
                forward_along(1)
            forward_across(0)

        @pl.when(odd & (half + 1 < line))
        def _():
            forward_along(half + 1)

        @pl.when(odd & (half < line))
        def _():
            forward_across(half)

        @pl.when(odd & (s >= 3))
        def _():
            to_partner(half - 1)

        @pl.when((lax.rem(s, 2) == 0) & (s >= 4))
        def _():
            to_owner(half - 1)

        return carry

    lax.fori_loop(0, 2 * line, step, 0)
    to_partner(0)
    if line > 1:
        to_owner(line - 1)
    total = chip_sum(0)
    for d in range(1, line):
        line_copy(d).wait_recv()
        total = total + line_in[d].astype(f32)
    kg_ref[0] = total[0].astype(jnp.bfloat16)
    vg_ref[0] = total[1].astype(jnp.bfloat16)

    for d in range(1, line):
        kv_copy(dp, kv_line_send.at[d], peer(d)).wait_send()
        line_copy(d).wait_send()

    def drain(d, carry):
        kv_copy(along(d) * 2 + b, kv_par_send.at[d], partner()).wait_send()
        par_copy(d).wait_send()
        return carry

    lax.fori_loop(0, line, drain, 0)

    def drain_prefix(p, carry):
        kv_copy(p, kv_sib_send.at[p], sibling()).wait_send()
        sib_copy(p).wait_send()
        return carry

    lax.fori_loop(0, prefixes, drain_prefix, 0)


def place_kernel(cap, dq_ref, kg_ref, vg_ref, tp_ref, out_hbm, kg_out, vg_out, counts, sem, small):
    tiles = out_hbm.shape[0]
    prefixes = dq_ref.shape[0]
    base = lax.axis_index("dp") * tiles
    kg_copy = pltpu.make_async_copy(kg_ref, kg_out, small.at[0])
    vg_copy = pltpu.make_async_copy(vg_ref, vg_out, small.at[1])
    kg_copy.start()
    vg_copy.start()
    for p in range(prefixes):
        counts[p] = 0

    def place(t, carry):
        p = tp_ref[0, base + t]
        c = counts[p]
        counts[p] = c + 1
        pltpu.make_async_copy(dq_ref.at[p, c], out_hbm.at[t], sem.at[t]).start()
        return carry

    def finish(t, carry):
        pltpu.make_async_copy(dq_ref.at[0, 0], out_hbm.at[t], sem.at[t]).wait()
        return carry

    lax.fori_loop(0, tiles, place, 0)
    lax.fori_loop(0, tiles, finish, 0)
    kg_copy.wait()
    vg_copy.wait()


def stay(array):
    return pltpu.with_memory_space_constraint(array, pltpu.HBM)


def shards(
    queries, output_gradient, prefix_keys, prefix_values, tile_prefix, suffix_lse, suffix_dot
):
    prefixes = lax.axis_size("dp")
    pos_count = lax.axis_size("pos")
    tiles, rows, width = queries.shape
    _, block, dim = prefix_keys.shape
    heads = width // dim
    tile_rows = rows * pos_count
    cap = max(2, tiles // prefixes)
    line = prefixes // 2
    bf16, f32 = jnp.bfloat16, jnp.float32
    named = stay(tile_prefix.T)
    hbm_spec = pl.BlockSpec(memory_space=pltpu.HBM)
    smem_spec = pl.BlockSpec(memory_space=pltpu.SMEM)
    vmem_spec = pl.BlockSpec(memory_space=pltpu.VMEM)
    dma = pltpu.SemaphoreType.DMA
    pair = (2, block, dim)
    work = 10 * tiles * rows * width * block * pos_count
    dq, kg, vg = pl.pallas_call(
        functools.partial(exchange_kernel, cap),
        out_shape=(
            jax.ShapeDtypeStruct((prefixes, cap, rows, width), bf16),
            jax.ShapeDtypeStruct(prefix_keys.shape, bf16),
            jax.ShapeDtypeStruct(prefix_values.shape, bf16),
        ),
        in_specs=[hbm_spec] * 7,
        out_specs=(vmem_spec, vmem_spec, vmem_spec),
        scratch_shapes=[
            pltpu.SMEM(named.shape, jnp.int32),
            pltpu.VMEM((tiles, rows, width), bf16),
            pltpu.VMEM((tiles, rows, width), bf16),
            pltpu.VMEM((prefixes, pos_count) + pair, bf16),
            pltpu.VMEM((tiles, heads, tile_rows), f32),
            pltpu.VMEM((tiles, heads, tile_rows), f32),
            pltpu.VMEM((tiles, heads * rows), f32),
            pltpu.VMEM((tiles, heads * rows), f32),
            pltpu.SMEM((prefixes * cap,), jnp.int32),
            pltpu.VMEM((prefixes,) + pair, f32),
            pltpu.VMEM((prefixes,) + pair, bf16),
            pltpu.VMEM((prefixes,) + pair, bf16),
            pltpu.VMEM((line,) + pair, bf16),
            pltpu.VMEM((line,) + pair, bf16),
            pltpu.VMEM((line,) + pair, bf16),
            pltpu.VMEM((line,) + pair, bf16),
            dma((7,)),
            dma((prefixes, pos_count)),
            dma((prefixes,)),
            dma((line,)),
            dma((line,)),
            dma((prefixes,)),
            dma((prefixes,)),
            dma((line,)),
            dma((line,)),
            dma((line,)),
            dma((line,)),
        ],
        compiler_params=pltpu.CompilerParams(
            collective_id=0, has_side_effects=True, vmem_limit_bytes=48 << 20
        ),
        cost_estimate=pl.CostEstimate(
            flops=work, bytes_accessed=6 * tiles * rows * width, transcendentals=0
        ),
        name="prefix_grads",
    )(
        stay(queries), stay(output_gradient), stay(prefix_keys), stay(prefix_values), named,
        stay(jnp.swapaxes(suffix_lse, 1, 2)), stay(jnp.swapaxes(suffix_dot, 1, 2)),
    )
    return pl.pallas_call(
        functools.partial(place_kernel, cap),
        out_shape=(
            jax.ShapeDtypeStruct(queries.shape, bf16),
            jax.ShapeDtypeStruct(prefix_keys.shape, bf16),
            jax.ShapeDtypeStruct(prefix_values.shape, bf16),
        ),
        in_specs=[vmem_spec] * 3 + [smem_spec],
        out_specs=(hbm_spec,) * 3,
        scratch_shapes=[pltpu.SMEM((prefixes,), jnp.int32), dma((tiles,)), dma((2,))],
        compiler_params=pltpu.CompilerParams(vmem_limit_bytes=16 << 20),
        name="place_tiles",
    )(dq, kg, vg, named)


def solution(mesh):
    in_specs = (
        P("dp", "pos", "head"),
        P("dp", "pos", "head"),
        P("dp", "pos", "head"),
        P("dp", "pos", "head"),
        P(),
        P(None, None, "head"),
        P(None, None, "head"),
    )
    out_specs = (P("dp", "pos", "head"), P("dp", "pos", "head"), P("dp", "pos", "head"))
    return jax.shard_map(shards, mesh=mesh, in_specs=in_specs, out_specs=out_specs, check_vma=False)
```

```python
import functools
import math

import jax
import jax.numpy as jnp
from jax import lax
from jax.experimental import pallas as pl
from jax.experimental.pallas import tpu as pltpu
from jax.sharding import PartitionSpec as P

MESH = pl.DeviceIdType.MESH
LOG2E = 1.0 / math.log(2.0)


def exchange_kernel(
    cap,
    q_hbm, g_hbm, k_hbm, v_hbm, tp_hbm, lse_hbm, dot_hbm,
    dq_ref, kg_ref, vg_ref,
    tp_ref, q_ref, g_ref, kv, lse_raw, dot_raw, lse_rows, dot_rows, slots,
    part, sib_out, sib_in, par_out, par_in, line_out, line_in,
    in_sem, kv_recv, kv_sib_send, kv_par_send, kv_line_send,
    sib_send, sib_recv, par_send, par_recv, line_send, line_recv,
):
    tiles, rows, width = q_ref.shape
    prefixes, pos_count, _, block, dim = kv.shape
    heads = width // dim
    line = prefixes // 2
    dp, pos = lax.axis_index("dp"), lax.axis_index("pos")
    a, b = dp // 2, lax.rem(dp, 2)
    other = 1 - b
    scaling = dim ** (-0.5)
    full = cap * prefixes == tiles

    def sibling():
        return {"pos": 1 - pos}

    def partner():
        return {"dp": a * 2 + other}

    def along(d):
        return lax.rem(a + d, line)

    def peer(d):
        return {"dp": along(d) * 2 + b}

    base = dp * tiles
    loads = [
        pltpu.make_async_copy(k_hbm.at[0], kv.at[dp, pos, 0], in_sem.at[0]),
        pltpu.make_async_copy(v_hbm.at[0], kv.at[dp, pos, 1], in_sem.at[1]),
        pltpu.make_async_copy(q_hbm, q_ref, in_sem.at[2]),
        pltpu.make_async_copy(g_hbm, g_ref, in_sem.at[3]),
        pltpu.make_async_copy(lse_hbm.at[pl.ds(base, tiles)], lse_raw, in_sem.at[4]),
        pltpu.make_async_copy(dot_hbm.at[pl.ds(base, tiles)], dot_raw, in_sem.at[5]),
        pltpu.make_async_copy(tp_hbm, tp_ref, in_sem.at[6]),
    ]
    for load in loads:
        load.start()

    barrier = pltpu.get_barrier_semaphore()
    pl.semaphore_signal(barrier, inc=1, device_id=sibling(), device_id_type=MESH)
    pl.semaphore_signal(barrier, inc=1, device_id=partner(), device_id_type=MESH)
    for d in range(1, line):
        pl.semaphore_signal(barrier, inc=1, device_id=peer(d), device_id_type=MESH)
    pl.semaphore_wait(barrier, line + 1)

    def remote(src, dst, send, recv, device):
        return pltpu.make_async_remote_copy(
            src_ref=src, dst_ref=dst, send_sem=send, recv_sem=recv,
            device_id=device, device_id_type=MESH,
        )

    def kv_copy(p, send, device):
        mine = kv.at[p, pos]
        return remote(mine, mine, send, kv_recv.at[p, pos], device)

    def kv_wait(p, which):
        here = kv.at[p, which]
        remote(here, here, kv_sib_send.at[p], kv_recv.at[p, which], sibling()).wait_recv()

    loads[0].wait()
    loads[1].wait()
    def send_along(d):
        kv_copy(dp, kv_line_send.at[d], peer(d)).start()

    if line > 1:
        send_along(1)
    kv_copy(dp, kv_par_send.at[0], partner()).start()
    kv_copy(dp, kv_sib_send.at[dp], sibling()).start()

    loads[6].wait()

    def find(p, carry):
        def look(i, found):
            t = tiles - 1 - i
            hit = tp_ref[0, base + t] == p
            shifted = (t,) + found[:-1]
            return tuple(jnp.where(hit, new, old) for new, old in zip(shifted, found))

        found = lax.fori_loop(0, tiles, look, (jnp.int32(-1),) * cap, unroll=True)
        for c in range(cap):
            slots[p * cap + c] = found[c]
        return carry

    lax.fori_loop(0, prefixes, find, 0)

    for load in loads[2:6]:
        load.wait()
    for raw, flat in ((lse_raw, lse_rows), (dot_raw, dot_rows)):
        pieces = []
        for h in range(heads):
            row = raw[:, h, :]
            piece = row[:, :rows]
            for other_pos in range(1, pos_count):
                piece = jnp.where(
                    pos == other_pos, row[:, other_pos * rows:(other_pos + 1) * rows], piece
                )
            pieces.append(piece)
        flat[...] = jnp.concatenate(pieces, axis=1)

    if line > 2:
        send_along(2)

    def stacked(ref, t):
        tile = ref[t]
        return jnp.concatenate([tile[:, h * dim:(h + 1) * dim] for h in range(heads)], axis=0)

    nt = (((1,), (1,)), ((), ()))
    f32 = jnp.float32

    def compute(p):
        keys = jnp.concatenate([kv[p, i, 0] for i in range(pos_count)], axis=0)
        values = jnp.concatenate([kv[p, i, 1] for i in range(pos_count)], axis=0)
        named = [slots[p * cap + c] for c in range(cap)]
        found = [jnp.maximum(t, 0) for t in named]
        query = [stacked(q_ref, t) for t in found]
        grad = [stacked(g_ref, t) for t in found]
        probs, score_grad = [], []
        for c in range(cap):
            scores = lax.dot_general(keys, query[c], nt, preferred_element_type=f32)
            prob_grad = lax.dot_general(values, grad[c], nt, preferred_element_type=f32)
            suffix_l = lse_rows[pl.ds(found[c], 1), :] * LOG2E
            suffix_d = dot_rows[pl.ds(found[c], 1), :]
            scores = scores * (scaling * LOG2E)
            top = jnp.maximum(jnp.max(scores, axis=0, keepdims=True), suffix_l)
            shifted = jnp.exp2(scores - top)
            suffix_w = jnp.exp2(suffix_l - top)
            mass = jnp.sum(shifted, axis=0, keepdims=True) + suffix_w
            moment = jnp.sum(shifted * prob_grad, axis=0, keepdims=True) + suffix_w * suffix_d
            inverse = 1.0 / mass
            delta = moment * inverse
            if not full:
                inverse = jnp.where(named[c] >= 0, inverse, 0.0)
            weights = shifted * inverse
            probs.append(weights.astype(jnp.bfloat16))
            score_grad.append((weights * (prob_grad - delta)).astype(jnp.bfloat16))
        probs = jnp.concatenate(probs, axis=1)
        score_grad = jnp.concatenate(score_grad, axis=1)
        value_sum = jnp.dot(probs, jnp.concatenate(grad, axis=0), preferred_element_type=f32)
        key_sum = jnp.dot(score_grad, jnp.concatenate(query, axis=0), preferred_element_type=f32)
        key_sum = key_sum * scaling
        for i, total in enumerate((key_sum, value_sum)):
            low, high = total[:block], total[block:]
            part[p, i] = jnp.where(pos == 0, low, high)
            sib_out[p, i] = jnp.where(pos == 0, high, low).astype(jnp.bfloat16)
        remote(
            sib_out.at[p], sib_in.at[p], sib_send.at[p], sib_recv.at[p], sibling()
        ).start()
        query_part = jnp.dot(keys.T, score_grad, preferred_element_type=f32)
        query_part = (query_part * scaling).astype(jnp.bfloat16).T
        for c in range(cap):
            for h in range(heads):
                first = (c * heads + h) * rows
                dq_ref[p, c, :, h * dim:(h + 1) * dim] = query_part[first:first + rows]

    def sib_copy(p):
        return remote(sib_out.at[p], sib_in.at[p], sib_send.at[p], sib_recv.at[p], sibling())

    def par_copy(d):
        return remote(par_out.at[d], par_in.at[d], par_send.at[d], par_recv.at[d], partner())

    def line_copy(d):
        return remote(line_out.at[d], line_in.at[d], line_send.at[d], line_recv.at[d], peer(d))

    def to_partner(d):
        p = along(d) * 2 + other
        sib_copy(p).wait_recv()
        par_out[d] = (part[p] + sib_in[p].astype(f32)).astype(jnp.bfloat16)
        par_copy(d).start()

    def chip_sum(d):
        p = along(d) * 2 + b
        sib_copy(p).wait_recv()
        par_copy(d).wait_recv()
        return part[p] + sib_in[p].astype(f32) + par_in[d].astype(f32)

    def to_owner(d):
        line_out[d] = chip_sum(d).astype(jnp.bfloat16)
        line_copy(d).start()

    def forward_along(d):
        p = along(d) * 2 + b
        kv_wait(p, pos)
        kv_copy(p, kv_par_send.at[d], partner()).start()
        kv_copy(p, kv_sib_send.at[p], sibling()).start()

    def forward_across(d):
        p = along(d) * 2 + other
        kv_wait(p, pos)
        kv_copy(p, kv_sib_send.at[p], sibling()).start()

    def step(s, carry):
        half = (s + 1) // 2
        odd = lax.rem(s, 2) == 1
        across = ((s > 0) & (lax.rem(s, 2) == 0)) | (s == 2 * line - 1)
        p = along(lax.rem(half, line)) * 2 + jnp.where(across, other, b)
        kv_wait(p, 1 - pos)
        compute(p)

        @pl.when(s == 0)
        def _():
            for d in range(3, line):
                send_along(d)
            forward_across(0)

        @pl.when(s + 1 < line)
        def _():
            forward_along(s + 1)

        @pl.when((s == 1) & (line > 1))
        def _():
            forward_across(1)

        @pl.when((lax.rem(s, 2) == 0) & (s >= 2) & (half + 1 < line))
        def _():
            forward_across(half + 1)

        @pl.when(odd & (s >= 3))
        def _():
            to_partner(half - 1)

        @pl.when((lax.rem(s, 2) == 0) & (s >= 4))
        def _():
            to_owner(half - 1)

        return carry

    lax.fori_loop(0, 2 * line, step, 0)
    to_partner(0)
    if line > 1:
        to_owner(line - 1)
    total = chip_sum(0)
    for d in range(1, line):
        line_copy(d).wait_recv()
        total = total + line_in[d].astype(f32)
    kg_ref[0] = total[0].astype(jnp.bfloat16)
    vg_ref[0] = total[1].astype(jnp.bfloat16)

    for d in range(1, line):
        kv_copy(dp, kv_line_send.at[d], peer(d)).wait_send()
        line_copy(d).wait_send()

    def drain(d, carry):
        kv_copy(along(d) * 2 + b, kv_par_send.at[d], partner()).wait_send()
        par_copy(d).wait_send()
        return carry

    lax.fori_loop(0, line, drain, 0)

    def drain_prefix(p, carry):
        kv_copy(p, kv_sib_send.at[p], sibling()).wait_send()
        sib_copy(p).wait_send()
        return carry

    lax.fori_loop(0, prefixes, drain_prefix, 0)


def place_kernel(cap, dq_ref, kg_ref, vg_ref, tp_ref, out_hbm, kg_out, vg_out, counts, sem, small):
    tiles = out_hbm.shape[0]
    prefixes = dq_ref.shape[0]
    base = lax.axis_index("dp") * tiles
    kg_copy = pltpu.make_async_copy(kg_ref, kg_out, small.at[0])
    vg_copy = pltpu.make_async_copy(vg_ref, vg_out, small.at[1])
    kg_copy.start()
    vg_copy.start()
    for p in range(prefixes):
        counts[p] = 0

    def place(t, carry):
        p = tp_ref[0, base + t]
        c = counts[p]
        counts[p] = c + 1
        pltpu.make_async_copy(dq_ref.at[p, c], out_hbm.at[t], sem.at[t]).start()
        return carry

    def finish(t, carry):
        pltpu.make_async_copy(dq_ref.at[0, 0], out_hbm.at[t], sem.at[t]).wait()
        return carry

    lax.fori_loop(0, tiles, place, 0)
    lax.fori_loop(0, tiles, finish, 0)
    kg_copy.wait()
    vg_copy.wait()


def stay(array):
    return pltpu.with_memory_space_constraint(array, pltpu.HBM)


def shards(
    queries, output_gradient, prefix_keys, prefix_values, tile_prefix, suffix_lse, suffix_dot
):
    prefixes = lax.axis_size("dp")
    pos_count = lax.axis_size("pos")
    tiles, rows, width = queries.shape
    _, block, dim = prefix_keys.shape
    heads = width // dim
    tile_rows = rows * pos_count
    cap = max(2, tiles // prefixes)
    line = prefixes // 2
    bf16, f32 = jnp.bfloat16, jnp.float32
    named = stay(tile_prefix.T)
    hbm_spec = pl.BlockSpec(memory_space=pltpu.HBM)
    smem_spec = pl.BlockSpec(memory_space=pltpu.SMEM)
    vmem_spec = pl.BlockSpec(memory_space=pltpu.VMEM)
    dma = pltpu.SemaphoreType.DMA
    pair = (2, block, dim)
    work = 10 * tiles * rows * width * block * pos_count
    dq, kg, vg = pl.pallas_call(
        functools.partial(exchange_kernel, cap),
        out_shape=(
            jax.ShapeDtypeStruct((prefixes, cap, rows, width), bf16),
            jax.ShapeDtypeStruct(prefix_keys.shape, bf16),
            jax.ShapeDtypeStruct(prefix_values.shape, bf16),
        ),
        in_specs=[hbm_spec] * 7,
        out_specs=(vmem_spec, vmem_spec, vmem_spec),
        scratch_shapes=[
            pltpu.SMEM(named.shape, jnp.int32),
            pltpu.VMEM((tiles, rows, width), bf16),
            pltpu.VMEM((tiles, rows, width), bf16),
            pltpu.VMEM((prefixes, pos_count) + pair, bf16),
            pltpu.VMEM((tiles, heads, tile_rows), f32),
            pltpu.VMEM((tiles, heads, tile_rows), f32),
            pltpu.VMEM((tiles, heads * rows), f32),
            pltpu.VMEM((tiles, heads * rows), f32),
            pltpu.SMEM((prefixes * cap,), jnp.int32),
            pltpu.VMEM((prefixes,) + pair, f32),
            pltpu.VMEM((prefixes,) + pair, bf16),
            pltpu.VMEM((prefixes,) + pair, bf16),
            pltpu.VMEM((line,) + pair, bf16),
            pltpu.VMEM((line,) + pair, bf16),
            pltpu.VMEM((line,) + pair, bf16),
            pltpu.VMEM((line,) + pair, bf16),
            dma((7,)),
            dma((prefixes, pos_count)),
            dma((prefixes,)),
            dma((line,)),
            dma((line,)),
            dma((prefixes,)),
            dma((prefixes,)),
            dma((line,)),
            dma((line,)),
            dma((line,)),
            dma((line,)),
        ],
        compiler_params=pltpu.CompilerParams(
            collective_id=0, has_side_effects=True, vmem_limit_bytes=48 << 20
        ),
        cost_estimate=pl.CostEstimate(
            flops=work, bytes_accessed=6 * tiles * rows * width, transcendentals=0
        ),
        name="prefix_grads",
    )(
        stay(queries), stay(output_gradient), stay(prefix_keys), stay(prefix_values), named,
        stay(jnp.swapaxes(suffix_lse, 1, 2)), stay(jnp.swapaxes(suffix_dot, 1, 2)),
    )
    return pl.pallas_call(
        functools.partial(place_kernel, cap),
        out_shape=(
            jax.ShapeDtypeStruct(queries.shape, bf16),
            jax.ShapeDtypeStruct(prefix_keys.shape, bf16),
            jax.ShapeDtypeStruct(prefix_values.shape, bf16),
        ),
        in_specs=[vmem_spec] * 3 + [smem_spec],
        out_specs=(hbm_spec,) * 3,
        scratch_shapes=[pltpu.SMEM((prefixes,), jnp.int32), dma((tiles,)), dma((2,))],
        compiler_params=pltpu.CompilerParams(vmem_limit_bytes=16 << 20),
        name="place_tiles",
    )(dq, kg, vg, named)


def solution(mesh):
    in_specs = (
        P("dp", "pos", "head"),
        P("dp", "pos", "head"),
        P("dp", "pos", "head"),
        P("dp", "pos", "head"),
        P(),
        P(None, None, "head"),
        P(None, None, "head"),
    )
    out_specs = (P("dp", "pos", "head"), P("dp", "pos", "head"), P("dp", "pos", "head"))
    return jax.shard_map(shards, mesh=mesh, in_specs=in_specs, out_specs=out_specs, check_vma=False)
```

```python
import functools
import math

import jax
import jax.numpy as jnp
from jax import lax
from jax.experimental import pallas as pl
from jax.experimental.pallas import tpu as pltpu
from jax.sharding import PartitionSpec as P

MESH = pl.DeviceIdType.MESH
LOG2E = 1.0 / math.log(2.0)


def exchange_kernel(
    cap,
    q_hbm, g_hbm, k_hbm, v_hbm, tp_hbm, lse_hbm, dot_hbm,
    dq_ref, kg_ref, vg_ref,
    tp_ref, q_ref, g_ref, kv, lse_raw, dot_raw, lse_rows, dot_rows, slots,
    scores_ref, change_ref, probs_ref, score_grad_ref,
    part, sib_out, sib_in, par_out, par_in, line_out, line_in,
    in_sem, kv_recv, kv_sib_send, kv_par_send, kv_line_send,
    sib_send, sib_recv, par_send, par_recv, line_send, line_recv,
):
    tiles, rows, width = q_ref.shape
    prefixes, pos_count, _, block, dim = kv.shape
    heads = width // dim
    line = prefixes // 2
    dp, pos = lax.axis_index("dp"), lax.axis_index("pos")
    a, b = dp // 2, lax.rem(dp, 2)
    other = 1 - b
    scaling = dim ** (-0.5)
    full = cap * prefixes == tiles

    def sibling():
        return {"pos": 1 - pos}

    def partner():
        return {"dp": a * 2 + other}

    def along(d):
        return lax.rem(a + d, line)

    def peer(d):
        return {"dp": along(d) * 2 + b}

    base = dp * tiles
    loads = [
        pltpu.make_async_copy(k_hbm.at[0], kv.at[dp, pos, 0], in_sem.at[0]),
        pltpu.make_async_copy(v_hbm.at[0], kv.at[dp, pos, 1], in_sem.at[1]),
        pltpu.make_async_copy(q_hbm, q_ref, in_sem.at[2]),
        pltpu.make_async_copy(g_hbm, g_ref, in_sem.at[3]),
        pltpu.make_async_copy(lse_hbm.at[pl.ds(base, tiles)], lse_raw, in_sem.at[4]),
        pltpu.make_async_copy(dot_hbm.at[pl.ds(base, tiles)], dot_raw, in_sem.at[5]),
        pltpu.make_async_copy(tp_hbm, tp_ref, in_sem.at[6]),
    ]
    for load in loads:
        load.start()

    barrier = pltpu.get_barrier_semaphore()
    pl.semaphore_signal(barrier, inc=1, device_id=sibling(), device_id_type=MESH)
    pl.semaphore_signal(barrier, inc=1, device_id=partner(), device_id_type=MESH)
    for d in range(1, line):
        pl.semaphore_signal(barrier, inc=1, device_id=peer(d), device_id_type=MESH)
    pl.semaphore_wait(barrier, line + 1)

    def remote(src, dst, send, recv, device):
        return pltpu.make_async_remote_copy(
            src_ref=src, dst_ref=dst, send_sem=send, recv_sem=recv,
            device_id=device, device_id_type=MESH,
        )

    def kv_copy(p, send, device):
        mine = kv.at[p, pos]
        return remote(mine, mine, send, kv_recv.at[p, pos], device)

    def kv_wait(p, which):
        here = kv.at[p, which]
        remote(here, here, kv_sib_send.at[p], kv_recv.at[p, which], sibling()).wait_recv()

    loads[0].wait()
    loads[1].wait()
    def send_along(d):
        kv_copy(dp, kv_line_send.at[d], peer(d)).start()

    if line > 1:
        send_along(1)
    kv_copy(dp, kv_par_send.at[0], partner()).start()
    kv_copy(dp, kv_sib_send.at[dp], sibling()).start()

    loads[6].wait()

    def find(p, carry):
        def look(i, found):
            t = tiles - 1 - i
            hit = tp_ref[0, base + t] == p
            shifted = (t,) + found[:-1]
            return tuple(jnp.where(hit, new, old) for new, old in zip(shifted, found))

        found = lax.fori_loop(0, tiles, look, (jnp.int32(-1),) * cap, unroll=True)
        for c in range(cap):
            slots[p * cap + c] = found[c]
        return carry

    lax.fori_loop(0, prefixes, find, 0)

    for load in loads[2:6]:
        load.wait()
    for raw, flat in ((lse_raw, lse_rows), (dot_raw, dot_rows)):
        pieces = []
        for h in range(heads):
            row = raw[:, h, :]
            piece = row[:, :rows]
            for other_pos in range(1, pos_count):
                piece = jnp.where(
                    pos == other_pos, row[:, other_pos * rows:(other_pos + 1) * rows], piece
                )
            pieces.append(piece)
        flat[...] = jnp.concatenate(pieces, axis=1)

    if line > 2:
        send_along(2)

    def stacked(ref, t):
        tile = ref[t]
        return jnp.concatenate([tile[:, h * dim:(h + 1) * dim] for h in range(heads)], axis=0)

    nt = (((1,), (1,)), ((), ()))
    f32 = jnp.float32

    def compute(p):
        keys = jnp.concatenate([kv[p, i, 0] for i in range(pos_count)], axis=0)
        values = jnp.concatenate([kv[p, i, 1] for i in range(pos_count)], axis=0)
        named = [slots[p * cap + c] for c in range(cap)]
        found = [jnp.maximum(t, 0) for t in named]
        query = [stacked(q_ref, t) for t in found]
        grad = [stacked(g_ref, t) for t in found]
        count = heads * rows
        for c in range(cap):
            here = slice(c * count, (c + 1) * count)
            scores_ref[:, here] = lax.dot_general(keys, query[c], nt, preferred_element_type=f32)
            change_ref[:, here] = lax.dot_general(values, grad[c], nt, preferred_element_type=f32)
        for c in range(cap):
            suffix_l = lse_rows[pl.ds(found[c], 1), :]
            suffix_d = dot_rows[pl.ds(found[c], 1), :]
            for first in range(0, count, 128):
                lanes = slice(first, first + 128)
                here = slice(c * count + first, c * count + first + 128)
                scores = scores_ref[:, here]
                top = jnp.max(scores, axis=0, keepdims=True)
                top = jnp.maximum(top, suffix_l[:, lanes] * (1.0 / scaling))
                shifted = jnp.exp2((scores - top) * (scaling * LOG2E))
                suffix_w = jnp.exp2((suffix_l[:, lanes] * (1.0 / scaling) - top) * (scaling * LOG2E))
                mass = jnp.sum(shifted, axis=0, keepdims=True) + suffix_w
                moment = jnp.sum(shifted * change_ref[:, here], axis=0, keepdims=True)
                inverse = 1.0 / mass
                delta = (moment + suffix_w * suffix_d[:, lanes]) * inverse
                if not full:
                    inverse = jnp.where(named[c] >= 0, inverse, 0.0)
                weights = shifted * inverse
                probs_ref[:, here] = weights.astype(jnp.bfloat16)
                change = weights * (change_ref[:, here] - delta)
                score_grad_ref[:, here] = change.astype(jnp.bfloat16)
        probs, score_grad = probs_ref[...], score_grad_ref[...]
        value_sum = jnp.dot(probs, jnp.concatenate(grad, axis=0), preferred_element_type=f32)
        key_sum = jnp.dot(score_grad, jnp.concatenate(query, axis=0), preferred_element_type=f32)
        key_sum = key_sum * scaling
        for i, total in enumerate((key_sum, value_sum)):
            low, high = total[:block], total[block:]
            part[p, i] = jnp.where(pos == 0, low, high)
            sib_out[p, i] = jnp.where(pos == 0, high, low).astype(jnp.bfloat16)
        remote(
            sib_out.at[p], sib_in.at[p], sib_send.at[p], sib_recv.at[p], sibling()
        ).start()
        query_part = jnp.dot(keys.T, score_grad, preferred_element_type=f32)
        query_part = (query_part * scaling).astype(jnp.bfloat16).T
        for c in range(cap):
            for h in range(heads):
                first = (c * heads + h) * rows
                dq_ref[p, c, :, h * dim:(h + 1) * dim] = query_part[first:first + rows]

    def sib_copy(p):
        return remote(sib_out.at[p], sib_in.at[p], sib_send.at[p], sib_recv.at[p], sibling())

    def par_copy(d):
        return remote(par_out.at[d], par_in.at[d], par_send.at[d], par_recv.at[d], partner())

    def line_copy(d):
        return remote(line_out.at[d], line_in.at[d], line_send.at[d], line_recv.at[d], peer(d))

    def to_partner(d):
        p = along(d) * 2 + other
        sib_copy(p).wait_recv()
        par_out[d] = (part[p] + sib_in[p].astype(f32)).astype(jnp.bfloat16)
        par_copy(d).start()

    def chip_sum(d):
        p = along(d) * 2 + b
        sib_copy(p).wait_recv()
        par_copy(d).wait_recv()
        return part[p] + sib_in[p].astype(f32) + par_in[d].astype(f32)

    def to_owner(d):
        line_out[d] = chip_sum(d).astype(jnp.bfloat16)
        line_copy(d).start()

    def forward_along(d):
        p = along(d) * 2 + b
        kv_wait(p, pos)
        kv_copy(p, kv_par_send.at[d], partner()).start()
        kv_copy(p, kv_sib_send.at[p], sibling()).start()

    def forward_across(d):
        p = along(d) * 2 + other
        kv_wait(p, pos)
        kv_copy(p, kv_sib_send.at[p], sibling()).start()

    def step(s, carry):
        half = (s + 1) // 2
        odd = lax.rem(s, 2) == 1
        across = ((s > 0) & (lax.rem(s, 2) == 0)) | (s == 2 * line - 1)
        p = along(lax.rem(half, line)) * 2 + jnp.where(across, other, b)
        kv_wait(p, 1 - pos)
        compute(p)

        @pl.when(s == 0)
        def _():
            for d in range(3, line):
                send_along(d)
            forward_across(0)

        @pl.when(s + 1 < line)
        def _():
            forward_along(s + 1)

        @pl.when((s == 1) & (line > 1))
        def _():
            forward_across(1)

        @pl.when((lax.rem(s, 2) == 0) & (s >= 2) & (half + 1 < line))
        def _():
            forward_across(half + 1)

        @pl.when(odd & (s >= 3))
        def _():
            to_partner(half - 1)

        @pl.when((lax.rem(s, 2) == 0) & (s >= 4))
        def _():
            to_owner(half - 1)

        return carry

    lax.fori_loop(0, 2 * line, step, 0)
    to_partner(0)

    for d in range(1, line):
        kv_copy(dp, kv_line_send.at[d], peer(d)).wait_send()

    def drain(d, carry):
        kv_copy(along(d) * 2 + b, kv_par_send.at[d], partner()).wait_send()
        return carry

    def drain_prefix(p, carry):
        kv_copy(p, kv_sib_send.at[p], sibling()).wait_send()
        sib_copy(p).wait_send()
        return carry

    lax.fori_loop(0, line, drain, 0)
    lax.fori_loop(0, prefixes, drain_prefix, 0)
    if line > 1:
        to_owner(line - 1)
    for d in range(line):
        par_copy(d).wait_send()
    total = chip_sum(0)
    for d in range(1, line):
        line_copy(d).wait_recv()
        total = total + line_in[d].astype(f32)
    kg_ref[0] = total[0].astype(jnp.bfloat16)
    vg_ref[0] = total[1].astype(jnp.bfloat16)
    for d in range(1, line):
        line_copy(d).wait_send()


def place_kernel(cap, dq_ref, kg_ref, vg_ref, tp_ref, out_hbm, kg_out, vg_out, counts, sem, small):
    tiles = out_hbm.shape[0]
    prefixes = dq_ref.shape[0]
    base = lax.axis_index("dp") * tiles
    kg_copy = pltpu.make_async_copy(kg_ref, kg_out, small.at[0])
    vg_copy = pltpu.make_async_copy(vg_ref, vg_out, small.at[1])
    kg_copy.start()
    vg_copy.start()
    for p in range(prefixes):
        counts[p] = 0

    def place(t, carry):
        p = tp_ref[0, base + t]
        c = counts[p]
        counts[p] = c + 1
        pltpu.make_async_copy(dq_ref.at[p, c], out_hbm.at[t], sem.at[t]).start()
        return carry

    def finish(t, carry):
        pltpu.make_async_copy(dq_ref.at[0, 0], out_hbm.at[t], sem.at[t]).wait()
        return carry

    lax.fori_loop(0, tiles, place, 0)
    lax.fori_loop(0, tiles, finish, 0)
    kg_copy.wait()
    vg_copy.wait()


def stay(array):
    return pltpu.with_memory_space_constraint(array, pltpu.HBM)


def shards(
    queries, output_gradient, prefix_keys, prefix_values, tile_prefix, suffix_lse, suffix_dot
):
    prefixes = lax.axis_size("dp")
    pos_count = lax.axis_size("pos")
    tiles, rows, width = queries.shape
    _, block, dim = prefix_keys.shape
    heads = width // dim
    tile_rows = rows * pos_count
    cap = max(2, tiles // prefixes)
    line = prefixes // 2
    bf16, f32 = jnp.bfloat16, jnp.float32
    named = stay(tile_prefix.T)
    hbm_spec = pl.BlockSpec(memory_space=pltpu.HBM)
    smem_spec = pl.BlockSpec(memory_space=pltpu.SMEM)
    vmem_spec = pl.BlockSpec(memory_space=pltpu.VMEM)
    dma = pltpu.SemaphoreType.DMA
    pair = (2, block, dim)
    work = 10 * tiles * rows * width * block * pos_count
    dq, kg, vg = pl.pallas_call(
        functools.partial(exchange_kernel, cap),
        out_shape=(
            jax.ShapeDtypeStruct((prefixes, cap, rows, width), bf16),
            jax.ShapeDtypeStruct(prefix_keys.shape, bf16),
            jax.ShapeDtypeStruct(prefix_values.shape, bf16),
        ),
        in_specs=[hbm_spec] * 7,
        out_specs=(vmem_spec, vmem_spec, vmem_spec),
        scratch_shapes=[
            pltpu.SMEM(named.shape, jnp.int32),
            pltpu.VMEM((tiles, rows, width), bf16),
            pltpu.VMEM((tiles, rows, width), bf16),
            pltpu.VMEM((prefixes, pos_count) + pair, bf16),
            pltpu.VMEM((tiles, heads, tile_rows), f32),
            pltpu.VMEM((tiles, heads, tile_rows), f32),
            pltpu.VMEM((tiles, heads * rows), f32),
            pltpu.VMEM((tiles, heads * rows), f32),
            pltpu.SMEM((prefixes * cap,), jnp.int32),
            pltpu.VMEM((block * pos_count, cap * heads * rows), f32),
            pltpu.VMEM((block * pos_count, cap * heads * rows), f32),
            pltpu.VMEM((block * pos_count, cap * heads * rows), bf16),
            pltpu.VMEM((block * pos_count, cap * heads * rows), bf16),
            pltpu.VMEM((prefixes,) + pair, f32),
            pltpu.VMEM((prefixes,) + pair, bf16),
            pltpu.VMEM((prefixes,) + pair, bf16),
            pltpu.VMEM((line,) + pair, bf16),
            pltpu.VMEM((line,) + pair, bf16),
            pltpu.VMEM((line,) + pair, bf16),
            pltpu.VMEM((line,) + pair, bf16),
            dma((7,)),
            dma((prefixes, pos_count)),
            dma((prefixes,)),
            dma((line,)),
            dma((line,)),
            dma((prefixes,)),
            dma((prefixes,)),
            dma((line,)),
            dma((line,)),
            dma((line,)),
            dma((line,)),
        ],
        compiler_params=pltpu.CompilerParams(
            collective_id=0, has_side_effects=True, vmem_limit_bytes=48 << 20
        ),
        cost_estimate=pl.CostEstimate(
            flops=work, bytes_accessed=6 * tiles * rows * width, transcendentals=0
        ),
        name="prefix_grads",
    )(
        stay(queries), stay(output_gradient), stay(prefix_keys), stay(prefix_values), named,
        stay(jnp.swapaxes(suffix_lse, 1, 2)), stay(jnp.swapaxes(suffix_dot, 1, 2)),
    )
    return pl.pallas_call(
        functools.partial(place_kernel, cap),
        out_shape=(
            jax.ShapeDtypeStruct(queries.shape, bf16),
            jax.ShapeDtypeStruct(prefix_keys.shape, bf16),
            jax.ShapeDtypeStruct(prefix_values.shape, bf16),
        ),
        in_specs=[vmem_spec] * 3 + [smem_spec],
        out_specs=(hbm_spec,) * 3,
        scratch_shapes=[pltpu.SMEM((prefixes,), jnp.int32), dma((tiles,)), dma((2,))],
        compiler_params=pltpu.CompilerParams(vmem_limit_bytes=16 << 20),
        name="place_tiles",
    )(dq, kg, vg, named)


def solution(mesh):
    in_specs = (
        P("dp", "pos", "head"),
        P("dp", "pos", "head"),
        P("dp", "pos", "head"),
        P("dp", "pos", "head"),
        P(),
        P(None, None, "head"),
        P(None, None, "head"),
    )
    out_specs = (P("dp", "pos", "head"), P("dp", "pos", "head"), P("dp", "pos", "head"))
    return jax.shard_map(shards, mesh=mesh, in_specs=in_specs, out_specs=out_specs, check_vma=False)
```

```python
import functools
import math

import jax
import jax.numpy as jnp
from jax import lax
from jax.experimental import pallas as pl
from jax.experimental.pallas import tpu as pltpu
from jax.sharding import PartitionSpec as P

MESH = pl.DeviceIdType.MESH
LOG2E = 1.0 / math.log(2.0)


def neighbours(line):
    dp, pos = lax.axis_index("dp"), lax.axis_index("pos")
    a, b = dp // 2, lax.rem(dp, 2)
    sibling = {"pos": 1 - pos}
    partner = {"dp": a * 2 + 1 - b}

    def along(d):
        return lax.rem(a + d, line)

    def peer(d):
        return {"dp": along(d) * 2 + b}

    return dp, pos, b, sibling, partner, along, peer


def greet(line, sibling, partner, peer):
    barrier = pltpu.get_barrier_semaphore()
    pl.semaphore_signal(barrier, inc=1, device_id=sibling, device_id_type=MESH)
    pl.semaphore_signal(barrier, inc=1, device_id=partner, device_id_type=MESH)
    for d in range(1, line):
        pl.semaphore_signal(barrier, inc=1, device_id=peer(d), device_id_type=MESH)
    pl.semaphore_wait(barrier, line + 1)


def remote(src, dst, send, recv, device):
    return pltpu.make_async_remote_copy(
        src_ref=src, dst_ref=dst, send_sem=send, recv_sem=recv,
        device_id=device, device_id_type=MESH,
    )


def gather_kernel(k_hbm, v_hbm, out_ref, kv, in_sem, kv_recv, kv_sib_send, kv_par_send, kv_line_send):
    prefixes = kv.shape[0]
    line = prefixes // 2
    dp, pos, b, sibling, partner, along, peer = neighbours(line)
    loads = [
        pltpu.make_async_copy(k_hbm.at[0], kv.at[dp, pos, 0], in_sem.at[0]),
        pltpu.make_async_copy(v_hbm.at[0], kv.at[dp, pos, 1], in_sem.at[1]),
    ]
    for load in loads:
        load.start()
    greet(line, sibling, partner, peer)
    for load in loads:
        load.wait()

    def kv_copy(p, send, device):
        mine = kv.at[p, pos]
        return remote(mine, mine, send, kv_recv.at[p, pos], device)

    def kv_wait(p, which):
        here = kv.at[p, which]
        remote(here, here, kv_sib_send.at[p], kv_recv.at[p, which], sibling).wait_recv()

    for d in range(1, line):
        kv_copy(dp, kv_line_send.at[d], peer(d)).start()
    kv_copy(dp, kv_par_send.at[0], partner).start()
    kv_copy(dp, kv_sib_send.at[dp], sibling).start()

    def forward_along(d, carry):
        p = along(d) * 2 + b
        kv_wait(p, pos)
        kv_copy(p, kv_par_send.at[d], partner).start()
        kv_copy(p, kv_sib_send.at[p], sibling).start()
        return carry

    def forward_across(d, carry):
        p = along(d) * 2 + 1 - b
        kv_wait(p, pos)
        kv_copy(p, kv_sib_send.at[p], sibling).start()
        return carry

    lax.fori_loop(1, line, forward_along, 0)
    lax.fori_loop(0, line, forward_across, 0)

    def receive(p, carry):
        kv_wait(p, 1 - pos)
        return carry

    def drain(p, carry):
        kv_copy(p, kv_sib_send.at[p], sibling).wait_send()
        return carry

    lax.fori_loop(0, prefixes, receive, 0)
    lax.fori_loop(0, prefixes, drain, 0)
    for d in range(line):
        kv_copy(along(d) * 2 + b, kv_par_send.at[d], partner).wait_send()
    for d in range(1, line):
        kv_copy(dp, kv_line_send.at[d], peer(d)).wait_send()
    out_ref[...] = kv[...]


def product_kernel(
    cap,
    q_hbm, g_hbm, kv, tp_hbm, lse_hbm, dot_hbm,
    dq_hbm, part, sib_out,
    tp_ref, q_ref, g_ref, dq_ref, lse_raw, dot_raw, lse_rows, dot_rows, slots,
    scores_ref, change_ref, probs_ref, score_grad_ref,
    in_sem, dq_sem,
):
    tiles, rows, width = q_ref.shape
    prefixes, pos_count, _, block, dim = kv.shape
    heads = width // dim
    dp, pos = lax.axis_index("dp"), lax.axis_index("pos")
    scaling = dim ** (-0.5)
    full = cap * prefixes == tiles
    base = dp * tiles
    loads = [
        pltpu.make_async_copy(lse_hbm.at[pl.ds(base, tiles)], lse_raw, in_sem.at[0]),
        pltpu.make_async_copy(dot_hbm.at[pl.ds(base, tiles)], dot_raw, in_sem.at[1]),
        pltpu.make_async_copy(q_hbm, q_ref, in_sem.at[2]),
        pltpu.make_async_copy(g_hbm, g_ref, in_sem.at[3]),
    ]
    named_load = pltpu.make_async_copy(tp_hbm, tp_ref, in_sem.at[4])
    named_load.start()
    for load in loads:
        load.start()

    def out_copy(p, c, t):
        return pltpu.make_async_copy(dq_ref.at[p, c], dq_hbm.at[t], dq_sem.at[p, c])

    named_load.wait()

    def find(p, carry):
        def look(i, found):
            t = tiles - 1 - i
            hit = tp_ref[0, base + t] == p
            shifted = (t,) + found[:-1]
            return tuple(jnp.where(hit, new, old) for new, old in zip(shifted, found))

        found = lax.fori_loop(0, tiles, look, (jnp.int32(-1),) * cap, unroll=True)
        for c in range(cap):
            slots[p * cap + c] = found[c]
        return carry

    lax.fori_loop(0, prefixes, find, 0)

    for load in loads:
        load.wait()
    for raw, flat in ((lse_raw, lse_rows), (dot_raw, dot_rows)):
        pieces = []
        for h in range(heads):
            row = raw[:, h, :]
            piece = row[:, :rows]
            for other_pos in range(1, pos_count):
                piece = jnp.where(
                    pos == other_pos, row[:, other_pos * rows:(other_pos + 1) * rows], piece
                )
            pieces.append(piece)
        flat[...] = jnp.concatenate(pieces, axis=1)


    def stacked(ref, t):
        tile = ref[t]
        return jnp.concatenate([tile[:, h * dim:(h + 1) * dim] for h in range(heads)], axis=0)

    nt = (((1,), (1,)), ((), ()))
    f32 = jnp.float32

    def compute(p, carry):
        keys = jnp.concatenate([kv[p, i, 0] for i in range(pos_count)], axis=0)
        values = jnp.concatenate([kv[p, i, 1] for i in range(pos_count)], axis=0)
        named = [slots[p * cap + c] for c in range(cap)]
        found = [jnp.maximum(t, 0) for t in named]
        query = [stacked(q_ref, t) for t in found]
        grad = [stacked(g_ref, t) for t in found]
        count = heads * rows
        for c in range(cap):
            here = slice(c * count, (c + 1) * count)
            scores_ref[:, here] = lax.dot_general(keys, query[c], nt, preferred_element_type=f32)
            change_ref[:, here] = lax.dot_general(values, grad[c], nt, preferred_element_type=f32)
        for c in range(cap):
            suffix_l = lse_rows[pl.ds(found[c], 1), :]
            suffix_d = dot_rows[pl.ds(found[c], 1), :]
            for first in range(0, count, 128):
                lanes = slice(first, first + 128)
                here = slice(c * count + first, c * count + first + 128)
                scores = scores_ref[:, here]
                top = jnp.max(scores, axis=0, keepdims=True)
                top = jnp.maximum(top, suffix_l[:, lanes] * (1.0 / scaling))
                shifted = jnp.exp2((scores - top) * (scaling * LOG2E))
                suffix_w = jnp.exp2((suffix_l[:, lanes] * (1.0 / scaling) - top) * (scaling * LOG2E))
                mass = jnp.sum(shifted, axis=0, keepdims=True) + suffix_w
                moment = jnp.sum(shifted * change_ref[:, here], axis=0, keepdims=True)
                inverse = 1.0 / mass
                delta = (moment + suffix_w * suffix_d[:, lanes]) * inverse
                if not full:
                    inverse = jnp.where(named[c] >= 0, inverse, 0.0)
                weights = shifted * inverse
                probs_ref[:, here] = weights.astype(jnp.bfloat16)
                change = weights * (change_ref[:, here] - delta)
                score_grad_ref[:, here] = change.astype(jnp.bfloat16)
        probs, score_grad = probs_ref[...], score_grad_ref[...]
        value_sum = jnp.dot(probs, jnp.concatenate(grad, axis=0), preferred_element_type=f32)
        key_sum = jnp.dot(score_grad, jnp.concatenate(query, axis=0), preferred_element_type=f32)
        key_sum = key_sum * scaling
        for i, total in enumerate((key_sum, value_sum)):
            low, high = total[:block], total[block:]
            part[p, i] = jnp.where(pos == 0, low, high)
            sib_out[p, i] = jnp.where(pos == 0, high, low).astype(jnp.bfloat16)
        query_part = jnp.dot(keys.T, score_grad, preferred_element_type=f32)
        query_part = (query_part * scaling).astype(jnp.bfloat16).T
        for c in range(cap):
            for h in range(heads):
                first = (c * heads + h) * rows
                dq_ref[p, c, :, h * dim:(h + 1) * dim] = query_part[first:first + rows]

            @pl.when(named[c] >= 0)
            def _():
                out_copy(p, c, found[c]).start()

        return carry

    lax.fori_loop(0, prefixes, compute, 0)

    def finish(p, carry):
        for c in range(cap):
            t = slots[p * cap + c]

            @pl.when(t >= 0)
            def _():
                out_copy(p, c, jnp.maximum(t, 0)).wait()

        return carry

    lax.fori_loop(0, prefixes, finish, 0)


def reduce_kernel(
    part, sib_first, kg_ref, vg_ref,
    sib_out, sib_in, par_out, par_in, line_out, line_in,
    sib_send, sib_recv, par_send, par_recv, line_send, line_recv,
):
    prefixes = part.shape[0]
    line = prefixes // 2
    f32 = jnp.float32
    dp, pos, b, sibling, partner, along, peer = neighbours(line)
    sib_out[...] = sib_first[...]
    greet(line, sibling, partner, peer)

    def sib_copy(p):
        return remote(sib_out.at[p], sib_in.at[p], sib_send.at[p], sib_recv.at[p], sibling)

    def par_copy(d):
        return remote(par_out.at[d], par_in.at[d], par_send.at[d], par_recv.at[d], partner)

    def line_copy(d):
        return remote(line_out.at[d], line_in.at[d], line_send.at[d], line_recv.at[d], peer(d))

    def to_partner(d):
        p = along(d) * 2 + 1 - b
        sib_copy(p).wait_recv()
        par_out[d] = (part[p] + sib_in[p].astype(f32)).astype(jnp.bfloat16)
        par_copy(d).start()

    def chip_sum(d):
        p = along(d) * 2 + b
        sib_copy(p).wait_recv()
        par_copy(d).wait_recv()
        return part[p] + sib_in[p].astype(f32) + par_in[d].astype(f32)

    order = [d % line for d in range(1, line + 1)]
    for d in order:
        sib_copy(along(d) * 2 + 1 - b).start()
    for d in order:
        sib_copy(along(d) * 2 + b).start()
    for d in order:
        to_partner(d)
    for d in range(1, line):
        line_out[d] = chip_sum(d).astype(jnp.bfloat16)
        line_copy(d).start()
    for p in range(prefixes):
        sib_copy(p).wait_send()
    for d in range(line):
        par_copy(d).wait_send()
    total = chip_sum(0)
    for d in range(1, line):
        line_copy(d).wait_recv()
        total = total + line_in[d].astype(f32)
    kg_ref[0] = total[0].astype(jnp.bfloat16)
    vg_ref[0] = total[1].astype(jnp.bfloat16)
    for d in range(1, line):
        line_copy(d).wait_send()


def stay(array):
    return pltpu.with_memory_space_constraint(array, pltpu.HBM)


def shards(
    queries, output_gradient, prefix_keys, prefix_values, tile_prefix, suffix_lse, suffix_dot
):
    prefixes = lax.axis_size("dp")
    pos_count = lax.axis_size("pos")
    tiles, rows, width = queries.shape
    _, block, dim = prefix_keys.shape
    heads = width // dim
    tile_rows = rows * pos_count
    cap = max(2, tiles // prefixes)
    line = prefixes // 2
    bf16, f32 = jnp.bfloat16, jnp.float32
    hbm_spec = pl.BlockSpec(memory_space=pltpu.HBM)
    vmem_spec = pl.BlockSpec(memory_space=pltpu.VMEM)
    dma = pltpu.SemaphoreType.DMA
    pair = (2, block, dim)
    kv = pl.pallas_call(
        gather_kernel,
        out_shape=jax.ShapeDtypeStruct((prefixes, pos_count) + pair, bf16),
        in_specs=[hbm_spec] * 2,
        out_specs=vmem_spec,
        scratch_shapes=[
            pltpu.VMEM((prefixes, pos_count) + pair, bf16),
            dma((2,)),
            dma((prefixes, pos_count)),
            dma((prefixes,)),
            dma((line,)),
            dma((line,)),
        ],
        compiler_params=pltpu.CompilerParams(
            collective_id=0, has_side_effects=True, vmem_limit_bytes=24 << 20
        ),
        name="gather_prefixes",
    )(stay(prefix_keys), stay(prefix_values))
    wide = (block * pos_count, cap * heads * rows)
    query_grad, part, sib_out = pl.pallas_call(
        functools.partial(product_kernel, cap),
        out_shape=(
            jax.ShapeDtypeStruct(queries.shape, bf16),
            jax.ShapeDtypeStruct((prefixes,) + pair, f32),
            jax.ShapeDtypeStruct((prefixes,) + pair, bf16),
        ),
        in_specs=[hbm_spec] * 2 + [vmem_spec] + [hbm_spec] * 3,
        out_specs=(hbm_spec, vmem_spec, vmem_spec),
        scratch_shapes=[
            pltpu.SMEM(tile_prefix.shape[::-1], jnp.int32),
            pltpu.VMEM((tiles, rows, width), bf16),
            pltpu.VMEM((tiles, rows, width), bf16),
            pltpu.VMEM((prefixes, cap, rows, width), bf16),
            pltpu.VMEM((tiles, heads, tile_rows), f32),
            pltpu.VMEM((tiles, heads, tile_rows), f32),
            pltpu.VMEM((tiles, heads * rows), f32),
            pltpu.VMEM((tiles, heads * rows), f32),
            pltpu.SMEM((prefixes * cap,), jnp.int32),
            pltpu.VMEM(wide, f32),
            pltpu.VMEM(wide, f32),
            pltpu.VMEM(wide, bf16),
            pltpu.VMEM(wide, bf16),
            dma((5,)),
            dma((prefixes, cap)),
        ],
        compiler_params=pltpu.CompilerParams(vmem_limit_bytes=24 << 20),
        name="tile_products",
    )(
        stay(queries), stay(output_gradient), kv, stay(tile_prefix.T),
        stay(jnp.swapaxes(suffix_lse, 1, 2)), stay(jnp.swapaxes(suffix_dot, 1, 2)),
    )
    key_grad, value_grad = pl.pallas_call(
        reduce_kernel,
        out_shape=(
            jax.ShapeDtypeStruct(prefix_keys.shape, bf16),
            jax.ShapeDtypeStruct(prefix_values.shape, bf16),
        ),
        in_specs=[vmem_spec] * 2,
        out_specs=(vmem_spec, vmem_spec),
        scratch_shapes=[
            pltpu.VMEM((prefixes,) + pair, bf16),
            pltpu.VMEM((prefixes,) + pair, bf16),
            pltpu.VMEM((line,) + pair, bf16),
            pltpu.VMEM((line,) + pair, bf16),
            pltpu.VMEM((line,) + pair, bf16),
            pltpu.VMEM((line,) + pair, bf16),
        ] + [dma((prefixes,))] * 2 + [dma((line,))] * 4,
        compiler_params=pltpu.CompilerParams(
            collective_id=1, has_side_effects=True, vmem_limit_bytes=24 << 20
        ),
        name="reduce_grads",
    )(part, sib_out)
    return query_grad, key_grad, value_grad


def solution(mesh):
    in_specs = (
        P("dp", "pos", "head"),
        P("dp", "pos", "head"),
        P("dp", "pos", "head"),
        P("dp", "pos", "head"),
        P(),
        P(None, None, "head"),
        P(None, None, "head"),
    )
    out_specs = (P("dp", "pos", "head"), P("dp", "pos", "head"), P("dp", "pos", "head"))
    return jax.shard_map(shards, mesh=mesh, in_specs=in_specs, out_specs=out_specs, check_vma=False)
```

```python
import functools
import math

import jax
import jax.numpy as jnp
from jax import lax
from jax.experimental import pallas as pl
from jax.experimental.pallas import tpu as pltpu
from jax.sharding import PartitionSpec as P

MESH = pl.DeviceIdType.MESH
LOG2E = 1.0 / math.log(2.0)


def exchange_kernel(
    cap,
    q_hbm, g_hbm, k_hbm, v_hbm, tp_hbm, lse_hbm, dot_hbm,
    dq_ref, kg_ref, vg_ref,
    tp_ref, q_ref, g_ref, kv, lse_raw, dot_raw, lse_rows, dot_rows, slots,
    scores_ref, change_ref, probs_ref, score_grad_ref,
    part, sib_out, sib_in, par_out, par_in, line_out, line_in,
    in_sem, kv_recv, kv_sib_send, kv_par_send, kv_line_send,
    sib_send, sib_recv, par_send, par_recv, line_send, line_recv,
):
    tiles, rows, width = q_ref.shape
    prefixes, pos_count, _, block, dim = kv.shape
    heads = width // dim
    line = prefixes // 2
    dp, pos = lax.axis_index("dp"), lax.axis_index("pos")
    a, b = dp // 2, lax.rem(dp, 2)
    other = 1 - b
    scaling = dim ** (-0.5)
    full = cap * prefixes == tiles

    def sibling():
        return {"pos": 1 - pos}

    def partner():
        return {"dp": a * 2 + other}

    def along(d):
        return lax.rem(a + d, line)

    def peer(d):
        return {"dp": along(d) * 2 + b}

    base = dp * tiles
    loads = [
        pltpu.make_async_copy(k_hbm.at[0], kv.at[dp, pos, 0], in_sem.at[0]),
        pltpu.make_async_copy(v_hbm.at[0], kv.at[dp, pos, 1], in_sem.at[1]),
        pltpu.make_async_copy(q_hbm, q_ref, in_sem.at[2]),
        pltpu.make_async_copy(g_hbm, g_ref, in_sem.at[3]),
        pltpu.make_async_copy(lse_hbm.at[pl.ds(base, tiles)], lse_raw, in_sem.at[4]),
        pltpu.make_async_copy(dot_hbm.at[pl.ds(base, tiles)], dot_raw, in_sem.at[5]),
        pltpu.make_async_copy(tp_hbm, tp_ref, in_sem.at[6]),
    ]
    for load in loads:
        load.start()

    barrier = pltpu.get_barrier_semaphore()
    pl.semaphore_signal(barrier, inc=1, device_id=sibling(), device_id_type=MESH)
    pl.semaphore_signal(barrier, inc=1, device_id=partner(), device_id_type=MESH)
    for d in range(1, line):
        pl.semaphore_signal(barrier, inc=1, device_id=peer(d), device_id_type=MESH)
    pl.semaphore_wait(barrier, line + 1)

    def remote(src, dst, send, recv, device):
        return pltpu.make_async_remote_copy(
            src_ref=src, dst_ref=dst, send_sem=send, recv_sem=recv,
            device_id=device, device_id_type=MESH,
        )

    def kv_copy(p, send, device):
        mine = kv.at[p, pos]
        return remote(mine, mine, send, kv_recv.at[p, pos], device)

    def kv_wait(p, which):
        here = kv.at[p, which]
        remote(here, here, kv_sib_send.at[p], kv_recv.at[p, which], sibling()).wait_recv()

    loads[0].wait()
    loads[1].wait()
    def send_along(d):
        kv_copy(dp, kv_line_send.at[d], peer(d)).start()

    if line > 1:
        send_along(1)
    kv_copy(dp, kv_par_send.at[0], partner()).start()
    kv_copy(dp, kv_sib_send.at[dp], sibling()).start()

    loads[6].wait()

    def find(p, carry):
        def look(i, found):
            t = tiles - 1 - i
            hit = tp_ref[0, base + t] == p
            shifted = (t,) + found[:-1]
            return tuple(jnp.where(hit, new, old) for new, old in zip(shifted, found))

        found = lax.fori_loop(0, tiles, look, (jnp.int32(-1),) * cap, unroll=True)
        for c in range(cap):
            slots[p * cap + c] = found[c]
        return carry

    lax.fori_loop(0, prefixes, find, 0)

    for load in loads[2:6]:
        load.wait()
    for raw, flat in ((lse_raw, lse_rows), (dot_raw, dot_rows)):
        pieces = []
        for h in range(heads):
            row = raw[:, h, :]
            piece = row[:, :rows]
            for other_pos in range(1, pos_count):
                piece = jnp.where(
                    pos == other_pos, row[:, other_pos * rows:(other_pos + 1) * rows], piece
                )
            pieces.append(piece)
        flat[...] = jnp.concatenate(pieces, axis=1)

    if line > 2:
        send_along(2)

    def stacked(ref, t):
        tile = ref[t]
        return jnp.concatenate([tile[:, h * dim:(h + 1) * dim] for h in range(heads)], axis=0)

    nt = (((1,), (1,)), ((), ()))
    f32 = jnp.float32

    def compute(p):
        keys = jnp.concatenate([kv[p, i, 0] for i in range(pos_count)], axis=0)
        values = jnp.concatenate([kv[p, i, 1] for i in range(pos_count)], axis=0)
        named = [slots[p * cap + c] for c in range(cap)]
        found = [jnp.maximum(t, 0) for t in named]
        query = [stacked(q_ref, t) for t in found]
        grad = [stacked(g_ref, t) for t in found]
        count = heads * rows
        for c in range(cap):
            here = slice(c * count, (c + 1) * count)
            scores_ref[:, here] = lax.dot_general(keys, query[c], nt, preferred_element_type=f32)
            change_ref[:, here] = lax.dot_general(values, grad[c], nt, preferred_element_type=f32)
        for c in range(cap):
            suffix_l = lse_rows[pl.ds(found[c], 1), :]
            suffix_d = dot_rows[pl.ds(found[c], 1), :]
            for first in range(0, count, 128):
                lanes = slice(first, first + 128)
                here = slice(c * count + first, c * count + first + 128)
                scores = scores_ref[:, here]
                top = jnp.max(scores, axis=0, keepdims=True)
                top = jnp.maximum(top, suffix_l[:, lanes] * (1.0 / scaling))
                shifted = jnp.exp2((scores - top) * (scaling * LOG2E))
                suffix_w = jnp.exp2((suffix_l[:, lanes] * (1.0 / scaling) - top) * (scaling * LOG2E))
                mass = jnp.sum(shifted, axis=0, keepdims=True) + suffix_w
                moment = jnp.sum(shifted * change_ref[:, here], axis=0, keepdims=True)
                inverse = 1.0 / mass
                delta = (moment + suffix_w * suffix_d[:, lanes]) * inverse
                if not full:
                    inverse = jnp.where(named[c] >= 0, inverse, 0.0)
                weights = shifted * inverse
                probs_ref[:, here] = weights.astype(jnp.bfloat16)
                change = weights * (change_ref[:, here] - delta)
                score_grad_ref[:, here] = change.astype(jnp.bfloat16)
        probs, score_grad = probs_ref[...], score_grad_ref[...]
        value_sum = jnp.dot(probs, jnp.concatenate(grad, axis=0), preferred_element_type=f32)
        key_sum = jnp.dot(score_grad, jnp.concatenate(query, axis=0), preferred_element_type=f32)
        key_sum = key_sum * scaling
        for i, total in enumerate((key_sum, value_sum)):
            low, high = total[:block], total[block:]
            part[p, i] = jnp.where(pos == 0, low, high)
            sib_out[p, i] = jnp.where(pos == 0, high, low).astype(jnp.bfloat16)
        remote(
            sib_out.at[p], sib_in.at[p], sib_send.at[p], sib_recv.at[p], sibling()
        ).start()
        query_part = jnp.dot(keys.T, score_grad, preferred_element_type=f32)
        query_part = (query_part * scaling).astype(jnp.bfloat16).T
        for c in range(cap):
            for h in range(heads):
                first = (c * heads + h) * rows
                dq_ref[p, c, :, h * dim:(h + 1) * dim] = query_part[first:first + rows]

    def sib_copy(p):
        return remote(sib_out.at[p], sib_in.at[p], sib_send.at[p], sib_recv.at[p], sibling())

    def par_copy(d):
        return remote(par_out.at[d], par_in.at[d], par_send.at[d], par_recv.at[d], partner())

    def line_copy(d):
        return remote(line_out.at[d], line_in.at[d], line_send.at[d], line_recv.at[d], peer(d))

    def to_partner(d):
        p = along(d) * 2 + other
        sib_copy(p).wait_recv()
        par_out[d] = (part[p] + sib_in[p].astype(f32)).astype(jnp.bfloat16)
        par_copy(d).start()

    def chip_sum(d):
        p = along(d) * 2 + b
        sib_copy(p).wait_recv()
        par_copy(d).wait_recv()
        return part[p] + sib_in[p].astype(f32) + par_in[d].astype(f32)

    def to_owner(d):
        line_out[d] = chip_sum(d).astype(jnp.bfloat16)
        line_copy(d).start()

    def forward_along(d):
        p = along(d) * 2 + b
        kv_wait(p, pos)
        kv_copy(p, kv_par_send.at[d], partner()).start()
        kv_copy(p, kv_sib_send.at[p], sibling()).start()

    def forward_across(d):
        p = along(d) * 2 + other
        kv_wait(p, pos)
        kv_copy(p, kv_sib_send.at[p], sibling()).start()

    last = 2 * line - 2 if line > 1 else 2

    def step(s, carry):
        half = s // 2
        odd = lax.rem(s, 2) == 1
        across = (odd & (s < last)) | (s == last)
        p = along(half) * 2 + jnp.where(across, other, b)
        kv_wait(p, 1 - pos)
        compute(p)

        @pl.when(s == 0)
        def _():
            for d in range(3, line):
                send_along(d)
            forward_across(0)

        @pl.when(s + 1 < line)
        def _():
            forward_along(s + 1)

        @pl.when(odd & (s <= 3) & (half + 1 < line))
        def _():
            forward_across(half + 1)

        @pl.when((lax.rem(s, 2) == 0) & (s >= 4) & (half + 1 < line))
        def _():
            forward_across(half + 1)

        @pl.when((lax.rem(s, 2) == 0) & (s >= 2))
        def _():
            to_partner(half - 1)

        @pl.when((lax.rem(s, 2) == 0) & (s >= 6))
        def _():
            to_owner(half - 2)

        return carry

    lax.fori_loop(0, 2 * line, step, 0)
    to_partner(line - 1)
    if line > 2:
        to_owner(line - 2)

    for d in range(1, line):
        kv_copy(dp, kv_line_send.at[d], peer(d)).wait_send()

    def drain(d, carry):
        kv_copy(along(d) * 2 + b, kv_par_send.at[d], partner()).wait_send()
        return carry

    def drain_prefix(p, carry):
        kv_copy(p, kv_sib_send.at[p], sibling()).wait_send()
        sib_copy(p).wait_send()
        return carry

    lax.fori_loop(0, line, drain, 0)
    lax.fori_loop(0, prefixes, drain_prefix, 0)
    if line > 1:
        to_owner(line - 1)
    for d in range(line):
        par_copy(d).wait_send()
    total = chip_sum(0)
    for d in range(1, line):
        line_copy(d).wait_recv()
        total = total + line_in[d].astype(f32)
    kg_ref[0] = total[0].astype(jnp.bfloat16)
    vg_ref[0] = total[1].astype(jnp.bfloat16)
    for d in range(1, line):
        line_copy(d).wait_send()


def place_kernel(cap, dq_ref, kg_ref, vg_ref, tp_ref, out_hbm, kg_out, vg_out, counts, sem, small):
    tiles = out_hbm.shape[0]
    prefixes = dq_ref.shape[0]
    base = lax.axis_index("dp") * tiles
    kg_copy = pltpu.make_async_copy(kg_ref, kg_out, small.at[0])
    vg_copy = pltpu.make_async_copy(vg_ref, vg_out, small.at[1])
    kg_copy.start()
    vg_copy.start()
    for p in range(prefixes):
        counts[p] = 0

    def place(t, carry):
        p = tp_ref[0, base + t]
        c = counts[p]
        counts[p] = c + 1
        pltpu.make_async_copy(dq_ref.at[p, c], out_hbm.at[t], sem.at[t]).start()
        return carry

    def finish(t, carry):
        pltpu.make_async_copy(dq_ref.at[0, 0], out_hbm.at[t], sem.at[t]).wait()
        return carry

    lax.fori_loop(0, tiles, place, 0)
    lax.fori_loop(0, tiles, finish, 0)
    kg_copy.wait()
    vg_copy.wait()


def stay(array):
    return pltpu.with_memory_space_constraint(array, pltpu.HBM)


def shards(
    queries, output_gradient, prefix_keys, prefix_values, tile_prefix, suffix_lse, suffix_dot
):
    prefixes = lax.axis_size("dp")
    pos_count = lax.axis_size("pos")
    tiles, rows, width = queries.shape
    _, block, dim = prefix_keys.shape
    heads = width // dim
    tile_rows = rows * pos_count
    cap = max(2, tiles // prefixes)
    line = prefixes // 2
    bf16, f32 = jnp.bfloat16, jnp.float32
    named = stay(tile_prefix.T)
    hbm_spec = pl.BlockSpec(memory_space=pltpu.HBM)
    smem_spec = pl.BlockSpec(memory_space=pltpu.SMEM)
    vmem_spec = pl.BlockSpec(memory_space=pltpu.VMEM)
    dma = pltpu.SemaphoreType.DMA
    pair = (2, block, dim)
    work = 10 * tiles * rows * width * block * pos_count
    dq, kg, vg = pl.pallas_call(
        functools.partial(exchange_kernel, cap),
        out_shape=(
            jax.ShapeDtypeStruct((prefixes, cap, rows, width), bf16),
            jax.ShapeDtypeStruct(prefix_keys.shape, bf16),
            jax.ShapeDtypeStruct(prefix_values.shape, bf16),
        ),
        in_specs=[hbm_spec] * 7,
        out_specs=(vmem_spec, vmem_spec, vmem_spec),
        scratch_shapes=[
            pltpu.SMEM(named.shape, jnp.int32),
            pltpu.VMEM((tiles, rows, width), bf16),
            pltpu.VMEM((tiles, rows, width), bf16),
            pltpu.VMEM((prefixes, pos_count) + pair, bf16),
            pltpu.VMEM((tiles, heads, tile_rows), f32),
            pltpu.VMEM((tiles, heads, tile_rows), f32),
            pltpu.VMEM((tiles, heads * rows), f32),
            pltpu.VMEM((tiles, heads * rows), f32),
            pltpu.SMEM((prefixes * cap,), jnp.int32),
            pltpu.VMEM((block * pos_count, cap * heads * rows), f32),
            pltpu.VMEM((block * pos_count, cap * heads * rows), f32),
            pltpu.VMEM((block * pos_count, cap * heads * rows), bf16),
            pltpu.VMEM((block * pos_count, cap * heads * rows), bf16),
            pltpu.VMEM((prefixes,) + pair, f32),
            pltpu.VMEM((prefixes,) + pair, bf16),
            pltpu.VMEM((prefixes,) + pair, bf16),
            pltpu.VMEM((line,) + pair, bf16),
            pltpu.VMEM((line,) + pair, bf16),
            pltpu.VMEM((line,) + pair, bf16),
            pltpu.VMEM((line,) + pair, bf16),
            dma((7,)),
            dma((prefixes, pos_count)),
            dma((prefixes,)),
            dma((line,)),
            dma((line,)),
            dma((prefixes,)),
            dma((prefixes,)),
            dma((line,)),
            dma((line,)),
            dma((line,)),
            dma((line,)),
        ],
        compiler_params=pltpu.CompilerParams(
            collective_id=0, has_side_effects=True, vmem_limit_bytes=48 << 20
        ),
        cost_estimate=pl.CostEstimate(
            flops=work, bytes_accessed=6 * tiles * rows * width, transcendentals=0
        ),
        name="prefix_grads",
    )(
        stay(queries), stay(output_gradient), stay(prefix_keys), stay(prefix_values), named,
        stay(jnp.swapaxes(suffix_lse, 1, 2)), stay(jnp.swapaxes(suffix_dot, 1, 2)),
    )
    return pl.pallas_call(
        functools.partial(place_kernel, cap),
        out_shape=(
            jax.ShapeDtypeStruct(queries.shape, bf16),
            jax.ShapeDtypeStruct(prefix_keys.shape, bf16),
            jax.ShapeDtypeStruct(prefix_values.shape, bf16),
        ),
        in_specs=[vmem_spec] * 3 + [smem_spec],
        out_specs=(hbm_spec,) * 3,
        scratch_shapes=[pltpu.SMEM((prefixes,), jnp.int32), dma((tiles,)), dma((2,))],
        compiler_params=pltpu.CompilerParams(vmem_limit_bytes=16 << 20),
        name="place_tiles",
    )(dq, kg, vg, named)


def solution(mesh):
    in_specs = (
        P("dp", "pos", "head"),
        P("dp", "pos", "head"),
        P("dp", "pos", "head"),
        P("dp", "pos", "head"),
        P(),
        P(None, None, "head"),
        P(None, None, "head"),
    )
    out_specs = (P("dp", "pos", "head"), P("dp", "pos", "head"), P("dp", "pos", "head"))
    return jax.shard_map(shards, mesh=mesh, in_specs=in_specs, out_specs=out_specs, check_vma=False)
```

```python
import functools
import math

import jax
import jax.numpy as jnp
from jax import lax
from jax.experimental import pallas as pl
from jax.experimental.pallas import tpu as pltpu
from jax.sharding import PartitionSpec as P

MESH = pl.DeviceIdType.MESH
LOG2E = 1.0 / math.log(2.0)


def exchange_kernel(
    cap,
    q_hbm, g_hbm, k_hbm, v_hbm, tp_hbm, lse_hbm, dot_hbm,
    dq_ref, kg_ref, vg_ref,
    tp_ref, q_ref, g_ref, kv, lse_raw, dot_raw, lse_rows, dot_rows, slots,
    scores_ref, change_ref, probs_ref, score_grad_ref,
    part, sib_out, sib_in, par_out, par_in, line_out, line_in,
    in_sem, kv_recv, kv_sib_send, kv_par_send, kv_line_send,
    sib_send, sib_recv, par_send, par_recv, line_send, line_recv,
):
    tiles, rows, width = q_ref.shape
    prefixes, pos_count, _, block, dim = kv.shape
    heads = width // dim
    line = prefixes // 2
    dp, pos = lax.axis_index("dp"), lax.axis_index("pos")
    a, b = dp // 2, lax.rem(dp, 2)
    other = 1 - b
    scaling = dim ** (-0.5)
    full = cap * prefixes == tiles

    def sibling():
        return {"pos": 1 - pos}

    def partner():
        return {"dp": a * 2 + other}

    def along(d):
        offset = jnp.where(lax.rem(d, 2) == 1, (d + 1) // 2, line - d // 2)
        return lax.rem(a + offset, line)

    def peer(d):
        return {"dp": along(d) * 2 + b}

    base = dp * tiles
    loads = [
        pltpu.make_async_copy(k_hbm.at[0], kv.at[dp, pos, 0], in_sem.at[0]),
        pltpu.make_async_copy(v_hbm.at[0], kv.at[dp, pos, 1], in_sem.at[1]),
        pltpu.make_async_copy(q_hbm, q_ref, in_sem.at[2]),
        pltpu.make_async_copy(g_hbm, g_ref, in_sem.at[3]),
        pltpu.make_async_copy(lse_hbm.at[pl.ds(base, tiles)], lse_raw, in_sem.at[4]),
        pltpu.make_async_copy(dot_hbm.at[pl.ds(base, tiles)], dot_raw, in_sem.at[5]),
        pltpu.make_async_copy(tp_hbm, tp_ref, in_sem.at[6]),
    ]
    for load in loads:
        load.start()

    barrier = pltpu.get_barrier_semaphore()
    pl.semaphore_signal(barrier, inc=1, device_id=sibling(), device_id_type=MESH)
    pl.semaphore_signal(barrier, inc=1, device_id=partner(), device_id_type=MESH)
    for d in range(1, line):
        pl.semaphore_signal(barrier, inc=1, device_id=peer(d), device_id_type=MESH)
    pl.semaphore_wait(barrier, line + 1)

    def remote(src, dst, send, recv, device):
        return pltpu.make_async_remote_copy(
            src_ref=src, dst_ref=dst, send_sem=send, recv_sem=recv,
            device_id=device, device_id_type=MESH,
        )

    def kv_copy(p, send, device):
        mine = kv.at[p, pos]
        return remote(mine, mine, send, kv_recv.at[p, pos], device)

    def kv_wait(p, which):
        here = kv.at[p, which]
        remote(here, here, kv_sib_send.at[p], kv_recv.at[p, which], sibling()).wait_recv()

    loads[0].wait()
    loads[1].wait()
    def send_along(d):
        kv_copy(dp, kv_line_send.at[d], peer(d)).start()

    for d in range(1, min(line, 3)):
        send_along(d)
    kv_copy(dp, kv_par_send.at[0], partner()).start()
    kv_copy(dp, kv_sib_send.at[dp], sibling()).start()

    loads[6].wait()

    def find(p, carry):
        def look(i, found):
            t = tiles - 1 - i
            hit = tp_ref[0, base + t] == p
            shifted = (t,) + found[:-1]
            return tuple(jnp.where(hit, new, old) for new, old in zip(shifted, found))

        found = lax.fori_loop(0, tiles, look, (jnp.int32(-1),) * cap, unroll=True)
        for c in range(cap):
            slots[p * cap + c] = found[c]
        return carry

    lax.fori_loop(0, prefixes, find, 0)

    for load in loads[2:6]:
        load.wait()
    for raw, flat in ((lse_raw, lse_rows), (dot_raw, dot_rows)):
        pieces = []
        for h in range(heads):
            row = raw[:, h, :]
            piece = row[:, :rows]
            for other_pos in range(1, pos_count):
                piece = jnp.where(
                    pos == other_pos, row[:, other_pos * rows:(other_pos + 1) * rows], piece
                )
            pieces.append(piece)
        flat[...] = jnp.concatenate(pieces, axis=1)

    def stacked(ref, t):
        tile = ref[t]
        return jnp.concatenate([tile[:, h * dim:(h + 1) * dim] for h in range(heads)], axis=0)

    nt = (((1,), (1,)), ((), ()))
    f32 = jnp.float32

    def compute(p):
        keys = jnp.concatenate([kv[p, i, 0] for i in range(pos_count)], axis=0)
        values = jnp.concatenate([kv[p, i, 1] for i in range(pos_count)], axis=0)
        named = [slots[p * cap + c] for c in range(cap)]
        found = [jnp.maximum(t, 0) for t in named]
        query = [stacked(q_ref, t) for t in found]
        grad = [stacked(g_ref, t) for t in found]
        count = heads * rows
        for c in range(cap):
            here = slice(c * count, (c + 1) * count)
            scores_ref[:, here] = lax.dot_general(keys, query[c], nt, preferred_element_type=f32)
            change_ref[:, here] = lax.dot_general(values, grad[c], nt, preferred_element_type=f32)
        for c in range(cap):
            suffix_l = lse_rows[pl.ds(found[c], 1), :]
            suffix_d = dot_rows[pl.ds(found[c], 1), :]
            for first in range(0, count, 128):
                lanes = slice(first, first + 128)
                here = slice(c * count + first, c * count + first + 128)
                scores = scores_ref[:, here]
                top = jnp.max(scores, axis=0, keepdims=True)
                top = jnp.maximum(top, suffix_l[:, lanes] * (1.0 / scaling))
                shifted = jnp.exp2((scores - top) * (scaling * LOG2E))
                suffix_w = jnp.exp2((suffix_l[:, lanes] * (1.0 / scaling) - top) * (scaling * LOG2E))
                mass = jnp.sum(shifted, axis=0, keepdims=True) + suffix_w
                moment = jnp.sum(shifted * change_ref[:, here], axis=0, keepdims=True)
                inverse = 1.0 / mass
                delta = (moment + suffix_w * suffix_d[:, lanes]) * inverse
                if not full:
                    inverse = jnp.where(named[c] >= 0, inverse, 0.0)
                weights = shifted * inverse
                probs_ref[:, here] = weights.astype(jnp.bfloat16)
                change = weights * (change_ref[:, here] - delta)
                score_grad_ref[:, here] = change.astype(jnp.bfloat16)
        probs, score_grad = probs_ref[...], score_grad_ref[...]
        value_sum = jnp.dot(probs, jnp.concatenate(grad, axis=0), preferred_element_type=f32)
        key_sum = jnp.dot(score_grad, jnp.concatenate(query, axis=0), preferred_element_type=f32)
        key_sum = key_sum * scaling
        for i, total in enumerate((key_sum, value_sum)):
            low, high = total[:block], total[block:]
            part[p, i] = jnp.where(pos == 0, low, high)
            sib_out[p, i] = jnp.where(pos == 0, high, low).astype(jnp.bfloat16)
        remote(
            sib_out.at[p], sib_in.at[p], sib_send.at[p], sib_recv.at[p], sibling()
        ).start()
        query_part = jnp.dot(keys.T, score_grad, preferred_element_type=f32)
        query_part = (query_part * scaling).astype(jnp.bfloat16).T
        for c in range(cap):
            for h in range(heads):
                first = (c * heads + h) * rows
                dq_ref[p, c, :, h * dim:(h + 1) * dim] = query_part[first:first + rows]

    def sib_copy(p):
        return remote(sib_out.at[p], sib_in.at[p], sib_send.at[p], sib_recv.at[p], sibling())

    def par_copy(d):
        return remote(par_out.at[d], par_in.at[d], par_send.at[d], par_recv.at[d], partner())

    def line_copy(d):
        return remote(line_out.at[d], line_in.at[d], line_send.at[d], line_recv.at[d], peer(d))

    def to_partner(d):
        p = along(d) * 2 + other
        sib_copy(p).wait_recv()
        par_out[d] = (part[p] + sib_in[p].astype(f32)).astype(jnp.bfloat16)
        par_copy(d).start()

    def chip_sum(d):
        p = along(d) * 2 + b
        sib_copy(p).wait_recv()
        par_copy(d).wait_recv()
        return part[p] + sib_in[p].astype(f32) + par_in[d].astype(f32)

    def to_owner(d):
        line_out[d] = chip_sum(d).astype(jnp.bfloat16)
        line_copy(d).start()

    def forward_along(d):
        p = along(d) * 2 + b
        kv_wait(p, pos)
        kv_copy(p, kv_par_send.at[d], partner()).start()
        kv_copy(p, kv_sib_send.at[p], sibling()).start()

    def forward_across(d):
        p = along(d) * 2 + other
        kv_wait(p, pos)
        kv_copy(p, kv_sib_send.at[p], sibling()).start()

    last = 2 * line - 2 if line > 1 else 2

    def step(s, carry):
        half = s // 2
        odd = lax.rem(s, 2) == 1
        across = (odd & (s < last)) | (s == last)
        p = along(half) * 2 + jnp.where(across, other, b)
        kv_wait(p, 1 - pos)
        compute(p)

        @pl.when(s == 0)
        def _():
            for d in range(3, line):
                send_along(d)
            forward_across(0)

        @pl.when(s + 1 < line)
        def _():
            forward_along(s + 1)

        @pl.when(odd & (s <= 3) & (half + 1 < line))
        def _():
            forward_across(half + 1)

        @pl.when((lax.rem(s, 2) == 0) & (s >= 4) & (half + 1 < line))
        def _():
            forward_across(half + 1)

        @pl.when((lax.rem(s, 2) == 0) & (s >= 2))
        def _():
            to_partner(half - 1)

        @pl.when((lax.rem(s, 2) == 0) & (s >= 6))
        def _():
            to_owner(half - 2)

        return carry

    lax.fori_loop(0, 2 * line, step, 0)
    to_partner(line - 1)
    if line > 2:
        to_owner(line - 2)

    for d in range(1, line):
        kv_copy(dp, kv_line_send.at[d], peer(d)).wait_send()

    def drain(d, carry):
        kv_copy(along(d) * 2 + b, kv_par_send.at[d], partner()).wait_send()
        return carry

    def drain_prefix(p, carry):
        kv_copy(p, kv_sib_send.at[p], sibling()).wait_send()
        sib_copy(p).wait_send()
        return carry

    lax.fori_loop(0, line, drain, 0)
    lax.fori_loop(0, prefixes, drain_prefix, 0)
    if line > 1:
        to_owner(line - 1)
    for d in range(line):
        par_copy(d).wait_send()
    total = chip_sum(0)
    for d in range(1, line):
        line_copy(d).wait_recv()
        total = total + line_in[d].astype(f32)
    kg_ref[0] = total[0].astype(jnp.bfloat16)
    vg_ref[0] = total[1].astype(jnp.bfloat16)
    for d in range(1, line):
        line_copy(d).wait_send()


def place_kernel(cap, dq_ref, kg_ref, vg_ref, tp_ref, out_hbm, kg_out, vg_out, counts, sem, small):
    tiles = out_hbm.shape[0]
    prefixes = dq_ref.shape[0]
    base = lax.axis_index("dp") * tiles
    kg_copy = pltpu.make_async_copy(kg_ref, kg_out, small.at[0])
    vg_copy = pltpu.make_async_copy(vg_ref, vg_out, small.at[1])
    kg_copy.start()
    vg_copy.start()
    for p in range(prefixes):
        counts[p] = 0

    def place(t, carry):
        p = tp_ref[0, base + t]
        c = counts[p]
        counts[p] = c + 1
        pltpu.make_async_copy(dq_ref.at[p, c], out_hbm.at[t], sem.at[t]).start()
        return carry

    def finish(t, carry):
        pltpu.make_async_copy(dq_ref.at[0, 0], out_hbm.at[t], sem.at[t]).wait()
        return carry

    lax.fori_loop(0, tiles, place, 0)
    lax.fori_loop(0, tiles, finish, 0)
    kg_copy.wait()
    vg_copy.wait()


def stay(array):
    return pltpu.with_memory_space_constraint(array, pltpu.HBM)


def shards(
    queries, output_gradient, prefix_keys, prefix_values, tile_prefix, suffix_lse, suffix_dot
):
    prefixes = lax.axis_size("dp")
    pos_count = lax.axis_size("pos")
    tiles, rows, width = queries.shape
    _, block, dim = prefix_keys.shape
    heads = width // dim
    tile_rows = rows * pos_count
    cap = max(2, tiles // prefixes)
    line = prefixes // 2
    bf16, f32 = jnp.bfloat16, jnp.float32
    named = stay(tile_prefix.T)
    hbm_spec = pl.BlockSpec(memory_space=pltpu.HBM)
    smem_spec = pl.BlockSpec(memory_space=pltpu.SMEM)
    vmem_spec = pl.BlockSpec(memory_space=pltpu.VMEM)
    dma = pltpu.SemaphoreType.DMA
    pair = (2, block, dim)
    work = 10 * tiles * rows * width * block * pos_count
    dq, kg, vg = pl.pallas_call(
        functools.partial(exchange_kernel, cap),
        out_shape=(
            jax.ShapeDtypeStruct((prefixes, cap, rows, width), bf16),
            jax.ShapeDtypeStruct(prefix_keys.shape, bf16),
            jax.ShapeDtypeStruct(prefix_values.shape, bf16),
        ),
        in_specs=[hbm_spec] * 7,
        out_specs=(vmem_spec, vmem_spec, vmem_spec),
        scratch_shapes=[
            pltpu.SMEM(named.shape, jnp.int32),
            pltpu.VMEM((tiles, rows, width), bf16),
            pltpu.VMEM((tiles, rows, width), bf16),
            pltpu.VMEM((prefixes, pos_count) + pair, bf16),
            pltpu.VMEM((tiles, heads, tile_rows), f32),
            pltpu.VMEM((tiles, heads, tile_rows), f32),
            pltpu.VMEM((tiles, heads * rows), f32),
            pltpu.VMEM((tiles, heads * rows), f32),
            pltpu.SMEM((prefixes * cap,), jnp.int32),
            pltpu.VMEM((block * pos_count, cap * heads * rows), f32),
            pltpu.VMEM((block * pos_count, cap * heads * rows), f32),
            pltpu.VMEM((block * pos_count, cap * heads * rows), bf16),
            pltpu.VMEM((block * pos_count, cap * heads * rows), bf16),
            pltpu.VMEM((prefixes,) + pair, f32),
            pltpu.VMEM((prefixes,) + pair, bf16),
            pltpu.VMEM((prefixes,) + pair, bf16),
            pltpu.VMEM((line,) + pair, bf16),
            pltpu.VMEM((line,) + pair, bf16),
            pltpu.VMEM((line,) + pair, bf16),
            pltpu.VMEM((line,) + pair, bf16),
            dma((7,)),
            dma((prefixes, pos_count)),
            dma((prefixes,)),
            dma((line,)),
            dma((line,)),
            dma((prefixes,)),
            dma((prefixes,)),
            dma((line,)),
            dma((line,)),
            dma((line,)),
            dma((line,)),
        ],
        compiler_params=pltpu.CompilerParams(
            collective_id=0, has_side_effects=True, vmem_limit_bytes=48 << 20
        ),
        cost_estimate=pl.CostEstimate(
            flops=work, bytes_accessed=6 * tiles * rows * width, transcendentals=0
        ),
        name="prefix_grads",
    )(
        stay(queries), stay(output_gradient), stay(prefix_keys), stay(prefix_values), named,
        stay(jnp.swapaxes(suffix_lse, 1, 2)), stay(jnp.swapaxes(suffix_dot, 1, 2)),
    )
    return pl.pallas_call(
        functools.partial(place_kernel, cap),
        out_shape=(
            jax.ShapeDtypeStruct(queries.shape, bf16),
            jax.ShapeDtypeStruct(prefix_keys.shape, bf16),
            jax.ShapeDtypeStruct(prefix_values.shape, bf16),
        ),
        in_specs=[vmem_spec] * 3 + [smem_spec],
        out_specs=(hbm_spec,) * 3,
        scratch_shapes=[pltpu.SMEM((prefixes,), jnp.int32), dma((tiles,)), dma((2,))],
        compiler_params=pltpu.CompilerParams(vmem_limit_bytes=16 << 20),
        name="place_tiles",
    )(dq, kg, vg, named)


def solution(mesh):
    in_specs = (
        P("dp", "pos", "head"),
        P("dp", "pos", "head"),
        P("dp", "pos", "head"),
        P("dp", "pos", "head"),
        P(),
        P(None, None, "head"),
        P(None, None, "head"),
    )
    out_specs = (P("dp", "pos", "head"), P("dp", "pos", "head"), P("dp", "pos", "head"))
    return jax.shard_map(shards, mesh=mesh, in_specs=in_specs, out_specs=out_specs, check_vma=False)
```

```python
import functools
import math

import jax
import jax.numpy as jnp
from jax import lax
from jax.experimental import pallas as pl
from jax.experimental.pallas import tpu as pltpu
from jax.sharding import PartitionSpec as P

MESH = pl.DeviceIdType.MESH
LOG2E = 1.0 / math.log(2.0)


def exchange_kernel(
    cap,
    q_hbm, g_hbm, k_hbm, v_hbm, tp_hbm, lse_hbm, dot_hbm,
    out_ref, kg_ref, vg_ref,
    dq_ref, tp_ref, q_ref, g_ref, kv, lse_raw, dot_raw, lse_rows, dot_rows, slots,
    scores_ref, change_ref, probs_ref, score_grad_ref,
    part, sib_out, sib_in, par_out, par_in, line_out, line_in,
    in_sem, kv_recv, kv_sib_send, kv_par_send, kv_line_send,
    sib_send, sib_recv, par_send, par_recv, line_send, line_recv,
):
    tiles, rows, width = q_ref.shape
    prefixes, pos_count, _, block, dim = kv.shape
    heads = width // dim
    line = prefixes // 2
    dp, pos = lax.axis_index("dp"), lax.axis_index("pos")
    a, b = dp // 2, lax.rem(dp, 2)
    other = 1 - b
    scaling = dim ** (-0.5)
    full = cap * prefixes == tiles

    def sibling():
        return {"pos": 1 - pos}

    def partner():
        return {"dp": a * 2 + other}

    def along(d):
        offset = jnp.where(lax.rem(d, 2) == 1, (d + 1) // 2, line - d // 2)
        return lax.rem(a + offset, line)

    def peer(d):
        return {"dp": along(d) * 2 + b}

    base = dp * tiles
    loads = [
        pltpu.make_async_copy(k_hbm.at[0], kv.at[dp, pos, 0], in_sem.at[0]),
        pltpu.make_async_copy(v_hbm.at[0], kv.at[dp, pos, 1], in_sem.at[1]),
        pltpu.make_async_copy(q_hbm, q_ref, in_sem.at[2]),
        pltpu.make_async_copy(g_hbm, g_ref, in_sem.at[3]),
        pltpu.make_async_copy(lse_hbm.at[pl.ds(base, tiles)], lse_raw, in_sem.at[4]),
        pltpu.make_async_copy(dot_hbm.at[pl.ds(base, tiles)], dot_raw, in_sem.at[5]),
        pltpu.make_async_copy(tp_hbm, tp_ref, in_sem.at[6]),
    ]
    for load in loads:
        load.start()

    barrier = pltpu.get_barrier_semaphore()
    pl.semaphore_signal(barrier, inc=1, device_id=sibling(), device_id_type=MESH)
    pl.semaphore_signal(barrier, inc=1, device_id=partner(), device_id_type=MESH)
    for d in range(1, line):
        pl.semaphore_signal(barrier, inc=1, device_id=peer(d), device_id_type=MESH)
    pl.semaphore_wait(barrier, line + 1)

    def remote(src, dst, send, recv, device):
        return pltpu.make_async_remote_copy(
            src_ref=src, dst_ref=dst, send_sem=send, recv_sem=recv,
            device_id=device, device_id_type=MESH,
        )

    def kv_copy(p, send, device):
        mine = kv.at[p, pos]
        return remote(mine, mine, send, kv_recv.at[p, pos], device)

    def kv_wait(p, which):
        here = kv.at[p, which]
        remote(here, here, kv_sib_send.at[p], kv_recv.at[p, which], sibling()).wait_recv()

    loads[0].wait()
    loads[1].wait()
    def send_along(d):
        kv_copy(dp, kv_line_send.at[d], peer(d)).start()

    for d in range(1, min(line, 3)):
        send_along(d)
    kv_copy(dp, kv_par_send.at[0], partner()).start()
    kv_copy(dp, kv_sib_send.at[dp], sibling()).start()

    loads[6].wait()

    def find(p, carry):
        def look(i, found):
            t = tiles - 1 - i
            hit = tp_ref[0, base + t] == p
            shifted = (t,) + found[:-1]
            return tuple(jnp.where(hit, new, old) for new, old in zip(shifted, found))

        found = lax.fori_loop(0, tiles, look, (jnp.int32(-1),) * cap, unroll=True)
        for c in range(cap):
            slots[p * cap + c] = found[c]
        return carry

    lax.fori_loop(0, prefixes, find, 0)

    for load in loads[2:6]:
        load.wait()
    for raw, flat in ((lse_raw, lse_rows), (dot_raw, dot_rows)):
        pieces = []
        for h in range(heads):
            row = raw[:, h, :]
            piece = row[:, :rows]
            for other_pos in range(1, pos_count):
                piece = jnp.where(
                    pos == other_pos, row[:, other_pos * rows:(other_pos + 1) * rows], piece
                )
            pieces.append(piece)
        flat[...] = jnp.concatenate(pieces, axis=1)

    def stacked(ref, t):
        tile = ref[t]
        return jnp.concatenate([tile[:, h * dim:(h + 1) * dim] for h in range(heads)], axis=0)

    nt = (((1,), (1,)), ((), ()))
    f32 = jnp.float32

    def compute(p):
        keys = jnp.concatenate([kv[p, i, 0] for i in range(pos_count)], axis=0)
        values = jnp.concatenate([kv[p, i, 1] for i in range(pos_count)], axis=0)
        named = [slots[p * cap + c] for c in range(cap)]
        found = [jnp.maximum(t, 0) for t in named]
        query = [stacked(q_ref, t) for t in found]
        grad = [stacked(g_ref, t) for t in found]
        count = heads * rows
        for c in range(cap):
            here = slice(c * count, (c + 1) * count)
            scores_ref[:, here] = lax.dot_general(keys, query[c], nt, preferred_element_type=f32)
            change_ref[:, here] = lax.dot_general(values, grad[c], nt, preferred_element_type=f32)
        for c in range(cap):
            suffix_l = lse_rows[pl.ds(found[c], 1), :]
            suffix_d = dot_rows[pl.ds(found[c], 1), :]
            for first in range(0, count, 128):
                lanes = slice(first, first + 128)
                here = slice(c * count + first, c * count + first + 128)
                scores = scores_ref[:, here]
                top = jnp.max(scores, axis=0, keepdims=True)
                top = jnp.maximum(top, suffix_l[:, lanes] * (1.0 / scaling))
                shifted = jnp.exp2((scores - top) * (scaling * LOG2E))
                suffix_w = jnp.exp2((suffix_l[:, lanes] * (1.0 / scaling) - top) * (scaling * LOG2E))
                mass = jnp.sum(shifted, axis=0, keepdims=True) + suffix_w
                moment = jnp.sum(shifted * change_ref[:, here], axis=0, keepdims=True)
                inverse = 1.0 / mass
                delta = (moment + suffix_w * suffix_d[:, lanes]) * inverse
                if not full:
                    inverse = jnp.where(named[c] >= 0, inverse, 0.0)
                weights = shifted * inverse
                probs_ref[:, here] = weights.astype(jnp.bfloat16)
                change = weights * (change_ref[:, here] - delta)
                score_grad_ref[:, here] = change.astype(jnp.bfloat16)
        probs, score_grad = probs_ref[...], score_grad_ref[...]
        value_sum = jnp.dot(probs, jnp.concatenate(grad, axis=0), preferred_element_type=f32)
        key_sum = jnp.dot(score_grad, jnp.concatenate(query, axis=0), preferred_element_type=f32)
        key_sum = key_sum * scaling
        for i, total in enumerate((key_sum, value_sum)):
            low, high = total[:block], total[block:]
            part[p, i] = jnp.where(pos == 0, low, high)
            sib_out[p, i] = jnp.where(pos == 0, high, low).astype(jnp.bfloat16)
        remote(
            sib_out.at[p], sib_in.at[p], sib_send.at[p], sib_recv.at[p], sibling()
        ).start()
        query_part = jnp.dot(keys.T, score_grad, preferred_element_type=f32)
        query_part = (query_part * scaling).astype(jnp.bfloat16).T
        for c in range(cap):
            for h in range(heads):
                first = (c * heads + h) * rows
                dq_ref[p, c, :, h * dim:(h + 1) * dim] = query_part[first:first + rows]

    def sib_copy(p):
        return remote(sib_out.at[p], sib_in.at[p], sib_send.at[p], sib_recv.at[p], sibling())

    def par_copy(d):
        return remote(par_out.at[d], par_in.at[d], par_send.at[d], par_recv.at[d], partner())

    def line_copy(d):
        return remote(line_out.at[d], line_in.at[d], line_send.at[d], line_recv.at[d], peer(d))

    def to_partner(d):
        p = along(d) * 2 + other
        sib_copy(p).wait_recv()
        par_out[d] = (part[p] + sib_in[p].astype(f32)).astype(jnp.bfloat16)
        par_copy(d).start()

    def chip_sum(d):
        p = along(d) * 2 + b
        sib_copy(p).wait_recv()
        par_copy(d).wait_recv()
        return part[p] + sib_in[p].astype(f32) + par_in[d].astype(f32)

    def to_owner(d):
        line_out[d] = chip_sum(d).astype(jnp.bfloat16)
        line_copy(d).start()

    def forward_along(d):
        p = along(d) * 2 + b
        kv_wait(p, pos)
        kv_copy(p, kv_par_send.at[d], partner()).start()
        kv_copy(p, kv_sib_send.at[p], sibling()).start()

    def forward_across(d):
        p = along(d) * 2 + other
        kv_wait(p, pos)
        kv_copy(p, kv_sib_send.at[p], sibling()).start()

    last = 2 * line - 2 if line > 1 else 2

    def step(s, carry):
        half = s // 2
        odd = lax.rem(s, 2) == 1
        across = (odd & (s < last)) | (s == last)
        p = along(half) * 2 + jnp.where(across, other, b)
        kv_wait(p, 1 - pos)
        compute(p)

        @pl.when(s == 0)
        def _():
            for d in range(3, line):
                send_along(d)
            forward_across(0)

        @pl.when(s + 1 < line)
        def _():
            forward_along(s + 1)

        @pl.when(odd & (s <= 3) & (half + 1 < line))
        def _():
            forward_across(half + 1)

        @pl.when((lax.rem(s, 2) == 0) & (s >= 4) & (half + 1 < line))
        def _():
            forward_across(half + 1)

        @pl.when((lax.rem(s, 2) == 0) & (s >= 2))
        def _():
            to_partner(half - 1)

        @pl.when((lax.rem(s, 2) == 0) & (s >= 6))
        def _():
            to_owner(half - 2)

        return carry

    lax.fori_loop(0, 2 * line, step, 0)
    to_partner(line - 1)
    if line > 2:
        to_owner(line - 2)

    if line > 1:
        to_owner(line - 1)

    def place(t, carry):
        p = tp_ref[0, base + t]
        c = jnp.int32(0)
        for later in range(1, cap):
            c = c + jnp.where(slots[p * cap + later] == t, later, 0)
        out_ref[t] = dq_ref[p, c]
        return carry

    def drain(d, carry):
        kv_copy(along(d) * 2 + b, kv_par_send.at[d], partner()).wait_send()
        par_copy(d).wait_send()
        return carry

    def drain_prefix(p, carry):
        kv_copy(p, kv_sib_send.at[p], sibling()).wait_send()
        sib_copy(p).wait_send()
        return carry

    lax.fori_loop(0, tiles, place, 0)
    for d in range(1, line):
        kv_copy(dp, kv_line_send.at[d], peer(d)).wait_send()
    lax.fori_loop(0, line, drain, 0)
    lax.fori_loop(0, prefixes, drain_prefix, 0)
    total = chip_sum(0)
    for d in range(1, line):
        line_copy(d).wait_recv()
        total = total + line_in[d].astype(f32)
    kg_ref[0] = total[0].astype(jnp.bfloat16)
    vg_ref[0] = total[1].astype(jnp.bfloat16)
    for d in range(1, line):
        line_copy(d).wait_send()


def write_kernel(dq_ref, kg_ref, vg_ref, dq_hbm, kg_hbm, vg_hbm, sem):
    pieces = sem.shape[0] - 2
    tiles = dq_ref.shape[0] // pieces
    copies = [
        pltpu.make_async_copy(kg_ref, kg_hbm, sem.at[pieces]),
        pltpu.make_async_copy(vg_ref, vg_hbm, sem.at[pieces + 1]),
    ]
    for i in range(pieces):
        here = pl.ds(i * tiles, tiles)
        copies.append(pltpu.make_async_copy(dq_ref.at[here], dq_hbm.at[here], sem.at[i]))
    for copy in copies:
        copy.start()
    for copy in copies:
        copy.wait()


def stay(array):
    return pltpu.with_memory_space_constraint(array, pltpu.HBM)


def shards(
    queries, output_gradient, prefix_keys, prefix_values, tile_prefix, suffix_lse, suffix_dot
):
    prefixes = lax.axis_size("dp")
    pos_count = lax.axis_size("pos")
    tiles, rows, width = queries.shape
    _, block, dim = prefix_keys.shape
    heads = width // dim
    tile_rows = rows * pos_count
    cap = max(2, tiles // prefixes)
    line = prefixes // 2
    bf16, f32 = jnp.bfloat16, jnp.float32
    named = stay(tile_prefix.T)
    hbm_spec = pl.BlockSpec(memory_space=pltpu.HBM)
    vmem_spec = pl.BlockSpec(memory_space=pltpu.VMEM)
    dma = pltpu.SemaphoreType.DMA
    pair = (2, block, dim)
    work = 10 * tiles * rows * width * block * pos_count
    dq, kg, vg = pl.pallas_call(
        functools.partial(exchange_kernel, cap),
        out_shape=(
            jax.ShapeDtypeStruct(queries.shape, bf16),
            jax.ShapeDtypeStruct(prefix_keys.shape, bf16),
            jax.ShapeDtypeStruct(prefix_values.shape, bf16),
        ),
        in_specs=[hbm_spec] * 7,
        out_specs=(vmem_spec, vmem_spec, vmem_spec),
        scratch_shapes=[
            pltpu.VMEM((prefixes, cap, rows, width), bf16),
            pltpu.SMEM(named.shape, jnp.int32),
            pltpu.VMEM((tiles, rows, width), bf16),
            pltpu.VMEM((tiles, rows, width), bf16),
            pltpu.VMEM((prefixes, pos_count) + pair, bf16),
            pltpu.VMEM((tiles, heads, tile_rows), f32),
            pltpu.VMEM((tiles, heads, tile_rows), f32),
            pltpu.VMEM((tiles, heads * rows), f32),
            pltpu.VMEM((tiles, heads * rows), f32),
            pltpu.SMEM((prefixes * cap,), jnp.int32),
            pltpu.VMEM((block * pos_count, cap * heads * rows), f32),
            pltpu.VMEM((block * pos_count, cap * heads * rows), f32),
            pltpu.VMEM((block * pos_count, cap * heads * rows), bf16),
            pltpu.VMEM((block * pos_count, cap * heads * rows), bf16),
            pltpu.VMEM((prefixes,) + pair, f32),
            pltpu.VMEM((prefixes,) + pair, bf16),
            pltpu.VMEM((prefixes,) + pair, bf16),
            pltpu.VMEM((line,) + pair, bf16),
            pltpu.VMEM((line,) + pair, bf16),
            pltpu.VMEM((line,) + pair, bf16),
            pltpu.VMEM((line,) + pair, bf16),
            dma((7,)),
            dma((prefixes, pos_count)),
            dma((prefixes,)),
            dma((line,)),
            dma((line,)),
            dma((prefixes,)),
            dma((prefixes,)),
            dma((line,)),
            dma((line,)),
            dma((line,)),
            dma((line,)),
        ],
        compiler_params=pltpu.CompilerParams(
            collective_id=0, has_side_effects=True, vmem_limit_bytes=48 << 20
        ),
        cost_estimate=pl.CostEstimate(
            flops=work, bytes_accessed=6 * tiles * rows * width, transcendentals=0
        ),
        name="prefix_grads",
    )(
        stay(queries), stay(output_gradient), stay(prefix_keys), stay(prefix_values), named,
        stay(jnp.swapaxes(suffix_lse, 1, 2)), stay(jnp.swapaxes(suffix_dot, 1, 2)),
    )
    return pl.pallas_call(
        write_kernel,
        out_shape=(
            jax.ShapeDtypeStruct(queries.shape, bf16),
            jax.ShapeDtypeStruct(prefix_keys.shape, bf16),
            jax.ShapeDtypeStruct(prefix_values.shape, bf16),
        ),
        in_specs=[vmem_spec] * 3,
        out_specs=(hbm_spec,) * 3,
        scratch_shapes=[dma((math.gcd(tiles, 8) + 2,))],
        compiler_params=pltpu.CompilerParams(vmem_limit_bytes=16 << 20),
        name="write_results",
    )(dq, kg, vg)


def solution(mesh):
    in_specs = (
        P("dp", "pos", "head"),
        P("dp", "pos", "head"),
        P("dp", "pos", "head"),
        P("dp", "pos", "head"),
        P(),
        P(None, None, "head"),
        P(None, None, "head"),
    )
    out_specs = (P("dp", "pos", "head"), P("dp", "pos", "head"), P("dp", "pos", "head"))
    return jax.shard_map(shards, mesh=mesh, in_specs=in_specs, out_specs=out_specs, check_vma=False)
```

```python
import functools
import math

import jax
import jax.numpy as jnp
from jax import lax
from jax.experimental import pallas as pl
from jax.experimental.pallas import tpu as pltpu
from jax.sharding import PartitionSpec as P

MESH = pl.DeviceIdType.MESH
LOG2E = 1.0 / math.log(2.0)


def exchange_kernel(
    cap,
    q_hbm, g_hbm, k_hbm, v_hbm, tp_hbm, lse_hbm, dot_hbm,
    out_ref, kg_ref, vg_ref,
    dq_ref, tp_ref, q_ref, g_ref, kv, lse_raw, dot_raw, lse_rows, dot_rows, slots,
    scores_ref, change_ref, probs_ref, score_grad_ref,
    part, sib_out, sib_in, par_out, par_in, line_out, line_in,
    in_sem, kv_recv, kv_sib_send, kv_par_send, kv_line_send,
    sib_send, sib_recv, par_send, par_recv, line_send, line_recv,
):
    tiles, rows, width = q_ref.shape
    prefixes, pos_count, _, block, dim = kv.shape
    heads = width // dim
    line = prefixes // 2
    dp, pos = lax.axis_index("dp"), lax.axis_index("pos")
    a, b = dp // 2, lax.rem(dp, 2)
    other = 1 - b
    scaling = dim ** (-0.5)
    full = cap * prefixes == tiles

    def sibling():
        return {"pos": 1 - pos}

    def partner():
        return {"dp": a * 2 + other}

    def along(d):
        offset = jnp.where(lax.rem(d, 2) == 1, (d + 1) // 2, line - d // 2)
        return lax.rem(a + offset, line)

    def peer(d):
        return {"dp": along(d) * 2 + b}

    base = dp * tiles
    loads = [
        pltpu.make_async_copy(k_hbm.at[0], kv.at[dp, pos, 0], in_sem.at[0]),
        pltpu.make_async_copy(v_hbm.at[0], kv.at[dp, pos, 1], in_sem.at[1]),
        pltpu.make_async_copy(q_hbm, q_ref, in_sem.at[2]),
        pltpu.make_async_copy(g_hbm, g_ref, in_sem.at[3]),
        pltpu.make_async_copy(lse_hbm.at[pl.ds(base, tiles)], lse_raw, in_sem.at[4]),
        pltpu.make_async_copy(dot_hbm.at[pl.ds(base, tiles)], dot_raw, in_sem.at[5]),
        pltpu.make_async_copy(tp_hbm, tp_ref, in_sem.at[6]),
    ]
    for load in loads:
        load.start()

    barrier = pltpu.get_barrier_semaphore()
    pl.semaphore_signal(barrier, inc=1, device_id=sibling(), device_id_type=MESH)
    pl.semaphore_signal(barrier, inc=1, device_id=partner(), device_id_type=MESH)
    for d in range(1, line):
        pl.semaphore_signal(barrier, inc=1, device_id=peer(d), device_id_type=MESH)
    pl.semaphore_wait(barrier, line + 1)

    def remote(src, dst, send, recv, device):
        return pltpu.make_async_remote_copy(
            src_ref=src, dst_ref=dst, send_sem=send, recv_sem=recv,
            device_id=device, device_id_type=MESH,
        )

    def kv_copy(p, send, device):
        mine = kv.at[p, pos]
        return remote(mine, mine, send, kv_recv.at[p, pos], device)

    def kv_wait(p, which):
        here = kv.at[p, which]
        remote(here, here, kv_sib_send.at[p], kv_recv.at[p, which], sibling()).wait_recv()

    loads[0].wait()
    loads[1].wait()
    def send_along(d):
        kv_copy(dp, kv_line_send.at[d], peer(d)).start()

    for d in range(1, min(line, 3)):
        send_along(d)
    kv_copy(dp, kv_par_send.at[0], partner()).start()
    kv_copy(dp, kv_sib_send.at[dp], sibling()).start()

    loads[6].wait()

    def find(p, carry):
        def look(i, found):
            t = tiles - 1 - i
            hit = tp_ref[0, base + t] == p
            shifted = (t,) + found[:-1]
            return tuple(jnp.where(hit, new, old) for new, old in zip(shifted, found))

        found = lax.fori_loop(0, tiles, look, (jnp.int32(-1),) * cap, unroll=True)
        for c in range(cap):
            slots[p * cap + c] = found[c]
        return carry

    lax.fori_loop(0, prefixes, find, 0)

    for load in loads[2:6]:
        load.wait()
    for raw, flat in ((lse_raw, lse_rows), (dot_raw, dot_rows)):
        pieces = []
        for h in range(heads):
            row = raw[:, h, :]
            piece = row[:, :rows]
            for other_pos in range(1, pos_count):
                piece = jnp.where(
                    pos == other_pos, row[:, other_pos * rows:(other_pos + 1) * rows], piece
                )
            pieces.append(piece)
        flat[...] = jnp.concatenate(pieces, axis=1)

    def stacked(ref, t):
        tile = ref[t]
        return jnp.concatenate([tile[:, h * dim:(h + 1) * dim] for h in range(heads)], axis=0)

    nt = (((1,), (1,)), ((), ()))
    f32 = jnp.float32

    def compute(p):
        keys = jnp.concatenate([kv[p, i, 0] for i in range(pos_count)], axis=0)
        values = jnp.concatenate([kv[p, i, 1] for i in range(pos_count)], axis=0)
        named = [slots[p * cap + c] for c in range(cap)]
        found = [jnp.maximum(t, 0) for t in named]
        query = [stacked(q_ref, t) for t in found]
        grad = [stacked(g_ref, t) for t in found]
        count = heads * rows
        for c in range(cap):
            here = slice(c * count, (c + 1) * count)
            scores_ref[:, here] = lax.dot_general(keys, query[c], nt, preferred_element_type=f32)
            change_ref[:, here] = lax.dot_general(values, grad[c], nt, preferred_element_type=f32)
        for c in range(cap):
            suffix_l = lse_rows[pl.ds(found[c], 1), :]
            suffix_d = dot_rows[pl.ds(found[c], 1), :]
            for first in range(0, count, 128):
                lanes = slice(first, first + 128)
                here = slice(c * count + first, c * count + first + 128)
                scores = scores_ref[:, here]
                top = jnp.max(scores, axis=0, keepdims=True)
                top = jnp.maximum(top, suffix_l[:, lanes] * (1.0 / scaling))
                shifted = jnp.exp2((scores - top) * (scaling * LOG2E))
                suffix_w = jnp.exp2((suffix_l[:, lanes] * (1.0 / scaling) - top) * (scaling * LOG2E))
                mass = jnp.sum(shifted, axis=0, keepdims=True) + suffix_w
                moment = jnp.sum(shifted * change_ref[:, here], axis=0, keepdims=True)
                inverse = 1.0 / mass
                delta = (moment + suffix_w * suffix_d[:, lanes]) * inverse
                if not full:
                    inverse = jnp.where(named[c] >= 0, inverse, 0.0)
                weights = shifted * inverse
                probs_ref[:, here] = weights.astype(jnp.bfloat16)
                change = weights * (change_ref[:, here] - delta)
                score_grad_ref[:, here] = change.astype(jnp.bfloat16)
        probs, score_grad = probs_ref[...], score_grad_ref[...]
        value_sum = jnp.dot(probs, jnp.concatenate(grad, axis=0), preferred_element_type=f32)
        key_sum = jnp.dot(score_grad, jnp.concatenate(query, axis=0), preferred_element_type=f32)
        key_sum = key_sum * scaling
        for i, total in enumerate((key_sum, value_sum)):
            low, high = total[:block], total[block:]
            part[p, i] = jnp.where(pos == 0, low, high)
            sib_out[p, i] = jnp.where(pos == 0, high, low).astype(jnp.bfloat16)
        remote(
            sib_out.at[p], sib_in.at[p], sib_send.at[p], sib_recv.at[p], sibling()
        ).start()
        query_part = jnp.dot(keys.T, score_grad, preferred_element_type=f32)
        query_part = (query_part * scaling).astype(jnp.bfloat16).T
        for c in range(cap):
            for h in range(heads):
                first = (c * heads + h) * rows
                dq_ref[p, c, :, h * dim:(h + 1) * dim] = query_part[first:first + rows]

    def sib_copy(p):
        return remote(sib_out.at[p], sib_in.at[p], sib_send.at[p], sib_recv.at[p], sibling())

    def par_copy(d, i):
        return remote(
            par_out.at[d, i], par_in.at[d, i], par_send.at[d, i], par_recv.at[d, i], partner()
        )

    def line_copy(d, i):
        return remote(
            line_out.at[d, i], line_in.at[d, i], line_send.at[d, i], line_recv.at[d, i], peer(d)
        )

    def to_partner(d):
        p = along(d) * 2 + other
        sib_copy(p).wait_recv()
        for i in range(2):
            par_out[d, i] = (part[p, i] + sib_in[p, i].astype(f32)).astype(jnp.bfloat16)
            par_copy(d, i).start()

    def chip_sum(d, i):
        p = along(d) * 2 + b
        if i == 0:
            sib_copy(p).wait_recv()
        par_copy(d, i).wait_recv()
        return part[p, i] + sib_in[p, i].astype(f32) + par_in[d, i].astype(f32)

    def to_owner(d):
        for i in range(2):
            line_out[d, i] = chip_sum(d, i).astype(jnp.bfloat16)
            line_copy(d, i).start()

    def forward_along(d):
        p = along(d) * 2 + b
        kv_wait(p, pos)
        kv_copy(p, kv_par_send.at[d], partner()).start()
        kv_copy(p, kv_sib_send.at[p], sibling()).start()

    def forward_across(d):
        p = along(d) * 2 + other
        kv_wait(p, pos)
        kv_copy(p, kv_sib_send.at[p], sibling()).start()

    last = 2 * line - 2 if line > 1 else 2

    def step(s, carry):
        half = s // 2
        odd = lax.rem(s, 2) == 1
        across = (odd & (s < last)) | (s == last)
        p = along(half) * 2 + jnp.where(across, other, b)
        kv_wait(p, 1 - pos)
        compute(p)

        @pl.when(s == 0)
        def _():
            for d in range(3, line):
                send_along(d)
            forward_across(0)

        @pl.when(s + 1 < line)
        def _():
            forward_along(s + 1)

        @pl.when(odd & (s <= 3) & (half + 1 < line))
        def _():
            forward_across(half + 1)

        @pl.when((lax.rem(s, 2) == 0) & (s >= 4) & (half + 1 < line))
        def _():
            forward_across(half + 1)

        @pl.when((lax.rem(s, 2) == 0) & (s >= 2))
        def _():
            to_partner(half - 1)

        @pl.when((lax.rem(s, 2) == 0) & (s >= 6))
        def _():
            to_owner(half - 2)

        return carry

    lax.fori_loop(0, 2 * line, step, 0)
    to_partner(line - 1)
    if line > 2:
        to_owner(line - 2)

    if line > 1:
        to_owner(line - 1)

    def place(t, carry):
        p = tp_ref[0, base + t]
        c = jnp.int32(0)
        for later in range(1, cap):
            c = c + jnp.where(slots[p * cap + later] == t, later, 0)
        out_ref[t] = dq_ref[p, c]
        return carry

    def drain(d, carry):
        kv_copy(along(d) * 2 + b, kv_par_send.at[d], partner()).wait_send()
        for i in range(2):
            par_copy(d, i).wait_send()
        return carry

    def drain_prefix(p, carry):
        kv_copy(p, kv_sib_send.at[p], sibling()).wait_send()
        sib_copy(p).wait_send()
        return carry

    lax.fori_loop(0, tiles, place, 0)
    for d in range(1, line):
        kv_copy(dp, kv_line_send.at[d], peer(d)).wait_send()
    lax.fori_loop(0, line, drain, 0)
    lax.fori_loop(0, prefixes, drain_prefix, 0)
    for i, grad_ref in enumerate((kg_ref, vg_ref)):
        total = chip_sum(0, i)
        for d in range(1, line):
            line_copy(d, i).wait_recv()
            total = total + line_in[d, i].astype(f32)
        grad_ref[0] = total.astype(jnp.bfloat16)
    for d in range(1, line):
        for i in range(2):
            line_copy(d, i).wait_send()


def write_kernel(dq_ref, kg_ref, vg_ref, dq_hbm, kg_hbm, vg_hbm, sem):
    pieces = sem.shape[0] - 2
    tiles = dq_ref.shape[0] // pieces
    copies = [
        pltpu.make_async_copy(kg_ref, kg_hbm, sem.at[pieces]),
        pltpu.make_async_copy(vg_ref, vg_hbm, sem.at[pieces + 1]),
    ]
    for i in range(pieces):
        here = pl.ds(i * tiles, tiles)
        copies.append(pltpu.make_async_copy(dq_ref.at[here], dq_hbm.at[here], sem.at[i]))
    for copy in copies:
        copy.start()
    for copy in copies:
        copy.wait()


def stay(array):
    return pltpu.with_memory_space_constraint(array, pltpu.HBM)


def shards(
    queries, output_gradient, prefix_keys, prefix_values, tile_prefix, suffix_lse, suffix_dot
):
    prefixes = lax.axis_size("dp")
    pos_count = lax.axis_size("pos")
    tiles, rows, width = queries.shape
    _, block, dim = prefix_keys.shape
    heads = width // dim
    tile_rows = rows * pos_count
    cap = max(2, tiles // prefixes)
    line = prefixes // 2
    bf16, f32 = jnp.bfloat16, jnp.float32
    named = stay(tile_prefix.T)
    hbm_spec = pl.BlockSpec(memory_space=pltpu.HBM)
    vmem_spec = pl.BlockSpec(memory_space=pltpu.VMEM)
    dma = pltpu.SemaphoreType.DMA
    pair = (2, block, dim)
    work = 10 * tiles * rows * width * block * pos_count
    dq, kg, vg = pl.pallas_call(
        functools.partial(exchange_kernel, cap),
        out_shape=(
            jax.ShapeDtypeStruct(queries.shape, bf16),
            jax.ShapeDtypeStruct(prefix_keys.shape, bf16),
            jax.ShapeDtypeStruct(prefix_values.shape, bf16),
        ),
        in_specs=[hbm_spec] * 7,
        out_specs=(vmem_spec, vmem_spec, vmem_spec),
        scratch_shapes=[
            pltpu.VMEM((prefixes, cap, rows, width), bf16),
            pltpu.SMEM(named.shape, jnp.int32),
            pltpu.VMEM((tiles, rows, width), bf16),
            pltpu.VMEM((tiles, rows, width), bf16),
            pltpu.VMEM((prefixes, pos_count) + pair, bf16),
            pltpu.VMEM((tiles, heads, tile_rows), f32),
            pltpu.VMEM((tiles, heads, tile_rows), f32),
            pltpu.VMEM((tiles, heads * rows), f32),
            pltpu.VMEM((tiles, heads * rows), f32),
            pltpu.SMEM((prefixes * cap,), jnp.int32),
            pltpu.VMEM((block * pos_count, cap * heads * rows), f32),
            pltpu.VMEM((block * pos_count, cap * heads * rows), f32),
            pltpu.VMEM((block * pos_count, cap * heads * rows), bf16),
            pltpu.VMEM((block * pos_count, cap * heads * rows), bf16),
            pltpu.VMEM((prefixes,) + pair, f32),
            pltpu.VMEM((prefixes,) + pair, bf16),
            pltpu.VMEM((prefixes,) + pair, bf16),
            pltpu.VMEM((line,) + pair, bf16),
            pltpu.VMEM((line,) + pair, bf16),
            pltpu.VMEM((line,) + pair, bf16),
            pltpu.VMEM((line,) + pair, bf16),
            dma((7,)),
            dma((prefixes, pos_count)),
            dma((prefixes,)),
            dma((line,)),
            dma((line,)),
            dma((prefixes,)),
            dma((prefixes,)),
            dma((line, 2)),
            dma((line, 2)),
            dma((line, 2)),
            dma((line, 2)),
        ],
        compiler_params=pltpu.CompilerParams(
            collective_id=0, has_side_effects=True, vmem_limit_bytes=48 << 20
        ),
        cost_estimate=pl.CostEstimate(
            flops=work, bytes_accessed=6 * tiles * rows * width, transcendentals=0
        ),
        name="prefix_grads",
    )(
        stay(queries), stay(output_gradient), stay(prefix_keys), stay(prefix_values), named,
        stay(jnp.swapaxes(suffix_lse, 1, 2)), stay(jnp.swapaxes(suffix_dot, 1, 2)),
    )
    return pl.pallas_call(
        write_kernel,
        out_shape=(
            jax.ShapeDtypeStruct(queries.shape, bf16),
            jax.ShapeDtypeStruct(prefix_keys.shape, bf16),
            jax.ShapeDtypeStruct(prefix_values.shape, bf16),
        ),
        in_specs=[vmem_spec] * 3,
        out_specs=(hbm_spec,) * 3,
        scratch_shapes=[dma((math.gcd(tiles, 8) + 2,))],
        compiler_params=pltpu.CompilerParams(vmem_limit_bytes=16 << 20),
        name="write_results",
    )(dq, kg, vg)


def solution(mesh):
    in_specs = (
        P("dp", "pos", "head"),
        P("dp", "pos", "head"),
        P("dp", "pos", "head"),
        P("dp", "pos", "head"),
        P(),
        P(None, None, "head"),
        P(None, None, "head"),
    )
    out_specs = (P("dp", "pos", "head"), P("dp", "pos", "head"), P("dp", "pos", "head"))
    return jax.shard_map(shards, mesh=mesh, in_specs=in_specs, out_specs=out_specs, check_vma=False)
```
